32 devices in a mesh: brick: 4 (over y, x), bulk: 8 (over z, core).
Axes of the slice: x: 2, y: 2, z: 4, core: 2. Of those that a mesh axis runs over, the one named last changes fastest.
Arguments:
- amp_traces: float32 [64, 512, 256], P(None, ('bulk', 'brick')), may hold values from -6 to 6
- patch_owner: int32 [65536, 1], P(('brick', 'bulk')), may hold values from 0 to 7; in each aligned block of 2048 rows (0 to 2047, 2048 to 4095, ...) at most 1024 rows name the same one
- patch_fault: int32 [65536], P(('brick', 'bulk')), may hold values from 0 to 15
- patch_trace: int32 [65536], P(('brick', 'bulk')), may hold values from 0 to 1023
- patch_offset: int32 [65536], P(('brick', 'bulk')), may hold values from 0 to 128
Outputs:
- fault_attr: float32 [64, 512, 256], P('brick', 'bulk')
- fault_profile: float32 [512, 128], P(('brick', 'bulk'))
The draws below stay inside these ranges and needn't reach their ends.
Inputs may be any that keep to these rules, and one draw needn't show every extreme that they name: `patch_owner`: among the 2048 patches of one device, at most 1024 name the same owner, and in every draw some device has exactly 1024 patches with one owner.
All inputs are finite; a program needn't handle non-finite values.
Results may differ from the reference program's by a relative error of at most 0.0003.
Values sent between devices are 32-bit elements; how exact they have to be, the bound alone decides.
No kernel may reach another device: no remote copies, remote signals or barrier semaphores. Data moves between devices by JAX's collectives and lax.ppermute only.
A program may use at most 64 MiB of HBM per device.

```python
import math
import jax
import jax.numpy as jnp
import numpy as np
from jax import lax

CX = 16
CY = 64
NT = 256
PATCH = 128
P_DEV = 2048
F_DEV = 16
NX = 64
NY = 512
CAP = 1024
PATCHES = 65536
FAULTS = 512
N_BRICK = 4
N_BULK = 8


def touch_ends(drawn, stream_key, low, top_value):
    dims = drawn.shape
    spot = [jax.random.randint(jax.random.fold_in(stream_key, axis), (), 0, dims[axis]) for axis in range(len(dims))]
    drawn = drawn.at[tuple(spot)].set(low)
    longest = dims.index(max(dims))
    spot[longest] = (spot[longest] + 1) % dims[longest]
    return drawn.at[tuple(spot)].set(top_value)


def block_levels(own_key, extent, split, low, high):
    loudness, own = 1.0, jax.random.fold_in(own_key, 6)
    for dim, parts in split:
        heights = jnp.exp(jax.random.uniform(jax.random.fold_in(own, dim), (parts,), jnp.float32, low / len(split), high / len(split)))
        loudness = loudness * jnp.repeat(heights, extent[dim] // parts).reshape([-1 if axis == dim else 1 for axis in range(len(extent))])
    return loudness


def deal_out(own_key, own, number, rows, amount, top, reach, lean):
    sequence = jax.random.permutation(own_key, amount)
    packed, ordinary = portions_of(amount, rows * top, reach, lean, True), portions_of(amount, rows * top, reach, lean, False)
    places = jnp.arange(amount)

    def named(tallies, rotation):
        used = int((tallies > 0).sum())
        fixed = max(1, used // 4)
        moved = fixed + (places - fixed + rotation * (used - fixed)) % max(1, amount - fixed)
        return jnp.zeros((amount,), jnp.int32).at[sequence[jnp.where(places < fixed, places, moved)]].set(jnp.asarray(tallies, jnp.int32))

    tallies = jnp.where(number % 4 == 0, named(packed, number // 4), named(ordinary, number - number // 4 - 1))
    mixed = jax.random.permutation(jax.random.fold_in(own, 3), amount)
    donor, sink = mixed[0:amount // 2 * 2:2], mixed[1:amount // 2 * 2:2]
    margin = jnp.minimum(tallies[donor] - 1, reach - tallies[sink]) // 2
    margin = jnp.where((donor == sequence[0]) | (sink == sequence[0]) | (tallies[sink] == 0), 0, jnp.maximum(margin, 0))
    moved = jax.random.randint(jax.random.fold_in(own, 4), (amount // 2,), 0, 1 << 20) % (margin + 1)
    tallies = tallies.at[donor].add(-moved).at[sink].add(moved)
    labels = jnp.searchsorted(jnp.cumsum(tallies), jnp.arange(rows * top), side="right").astype(jnp.int32)
    table = labels.reshape(top, rows).T
    table = table[jax.random.permutation(jax.random.fold_in(own, 1), rows)]
    rotation = jax.random.randint(jax.random.fold_in(own, 2), (rows, 1), 0, top)
    return jnp.take_along_axis(table, (jnp.arange(top)[None, :] + rotation) % top, axis=1)


def portions_of(count, total, bound, skew, full):
    loads = [(1 << 20) // math.isqrt(grade ** skew) + 1 for grade in range(1, count + 1)]
    largest = bound if full else min(bound, max(-(-total // count), total * loads[0] // sum(loads)))
    least = 1 if total - largest >= count - 1 else 0
    holding, rest = [largest] + [least] * (count - 1), total - largest - least * (count - 1)
    while rest > 0:
        movable = [i for i in range(1, count) if holding[i] < largest] or [i for i in range(1, count) if holding[i] < bound]
        whole, remaining = sum([loads[i] for i in movable]), rest
        for i in movable:
            addition = min(bound - holding[i], max(1, remaining * loads[i] // whole), rest)
            holding[i] = holding[i] + addition
            rest = rest - addition
    return np.array(holding)


def centred(rng, extent, spread, reach, cuts=(), held_as=jnp.bfloat16):
    drawn = jax.random.normal(rng, extent, jnp.float32) * spread
    if len(cuts) > 0:
        drawn = block_levels(rng, extent, cuts, -0.22, 0.18) * drawn
    return jnp.clip(drawn, min=-reach, max=reach).astype(held_as)


def setup_inputs(seed: int = 0) -> dict:
    keys = jax.random.split(jax.random.key(seed), 6)
    amp_traces = centred(keys[0], (NX, NY, NT), 1.0, 6.0, ((1, 32),), jnp.float32)
    patch_owner_keys = jax.random.split(jax.random.fold_in(keys[1], 1), PATCHES // P_DEV)
    patch_owner_turns = jax.random.permutation(jax.random.fold_in(keys[1], 3), PATCHES // P_DEV)
    patch_owner = jax.vmap(lambda own, number: deal_out(jax.random.fold_in(keys[1], 2), own, number, P_DEV, N_BULK, 1, CAP, 2))(patch_owner_keys, patch_owner_turns).reshape((PATCHES, 1))
    patch_fault = touch_ends(jax.random.randint(keys[2], (PATCHES,), 0, F_DEV), jax.random.fold_in(keys[2], 1), 0, F_DEV - 1).astype(jnp.int32)
    patch_trace = touch_ends(jax.random.randint(keys[3], (PATCHES,), 0, CX * CY), jax.random.fold_in(keys[3], 1), 0, (CX * CY) - 1).astype(jnp.int32)
    patch_offset = touch_ends(jax.random.randint(keys[4], (PATCHES,), 0, NT - PATCH + 1), jax.random.fold_in(keys[4], 1), 0, NT - PATCH).astype(jnp.int32)
    return dict(amp_traces=amp_traces, patch_owner=patch_owner, patch_fault=patch_fault, patch_trace=patch_trace, patch_offset=patch_offset)


def box_sum(values, radius, dimension):
    length = values.shape[dimension] - 2 * radius
    summed = lax.slice_in_dim(values, 0, length, axis=dimension)
    for offset in range(1, 2 * radius + 1):
        summed = summed + lax.slice_in_dim(values, offset, offset + length, axis=dimension)
    return summed


def time_sum(values, radius):
    widths = [(0, 0)] * (values.ndim - 1) + [(radius, radius)]
    return box_sum(jnp.pad(values, widths), radius, values.ndim - 1)


def gradient_energy(padded):
    slope_inline = 0.5 * (padded[2:, 1:-1, :] - padded[:-2, 1:-1, :])
    slope_cross = 0.5 * (padded[1:-1, 2:, :] - padded[1:-1, :-2, :])
    centre = jnp.pad(padded[1:-1, 1:-1, :], ((0, 0), (0, 0), (1, 1)))
    slope_time = 0.5 * (centre[:, :, 2:] - centre[:, :, :-2])
    return jnp.stack([slope_inline * slope_inline, slope_cross * slope_cross, slope_time * slope_time])


def smooth_tensor(energy):
    return time_sum(box_sum(box_sum(energy, 2, 1), 2, 2), 2)


def finish(tensor, near_amp):
    lateral = (tensor[0] + tensor[1]) / (tensor[0] + tensor[1] + tensor[2] + 1e-5)
    stack = box_sum(box_sum(near_amp, 1, 0), 1, 1)
    power = box_sum(box_sum(near_amp * near_amp, 1, 0), 1, 1)
    semblance = time_sum(stack * stack, 4) / (9.0 * time_sum(power, 4) + 1e-5)
    return (1.0 - semblance) * lateral


def reference(amp_traces, patch_owner, patch_fault, patch_trace, patch_offset):
    padded = jnp.pad(amp_traces, ((3, 3), (3, 3), (0, 0)))
    cross_pos = jnp.arange(NY + 4, dtype=jnp.int32) - 2
    cross_ok = ((cross_pos >= 0) & (cross_pos < NY)).astype(jnp.float32)

    def slab_attribute(index):
        slab = lax.dynamic_slice_in_dim(padded, (index * CX).astype(jnp.int32), CX + 6, 0)
        inline_pos = index * CX - 2 + jnp.arange(CX + 4, dtype=jnp.int32)
        inline_ok = ((inline_pos >= 0) & (inline_pos < NX)).astype(jnp.float32)
        weight_mask = inline_ok[:, None, None] * cross_ok[None, :, None]
        energy = gradient_energy(slab) * weight_mask[None]
        return finish(smooth_tensor(energy), slab[2:-2, 2:-2, :])

    slabs = lax.map(slab_attribute, jnp.arange(N_BRICK, dtype=jnp.int32))
    attribute = slabs.reshape(NX, NY, NT)
    patch_ids = jnp.arange(PATCHES, dtype=jnp.int32)
    device = patch_ids // P_DEV
    brick_of = device // N_BULK
    bulk_of = device % N_BULK
    inline_at = brick_of * CX + patch_trace // CY
    cross_at = bulk_of * CY + patch_trace % CY
    sample_index = patch_offset[:, None] + jnp.arange(PATCH, dtype=jnp.int32)[None, :]
    patch_rows = attribute[inline_at[:, None], cross_at[:, None], sample_index]
    fault_ids = brick_of * (F_DEV * N_BULK) + patch_owner[:, 0] * F_DEV + patch_fault
    summed = jax.ops.segment_sum(patch_rows, fault_ids, num_segments=FAULTS)
    counts = jax.ops.segment_sum(jnp.ones((PATCHES,), jnp.float32), fault_ids, num_segments=FAULTS)
    profile = summed / jnp.maximum(counts, 1.0)[:, None]
    return attribute, profile
```

```python
import jax
import jax.numpy as jnp
from jax import lax
from jax.experimental import pallas as pl
from jax.experimental.pallas import tpu as pltpu
from jax.sharding import PartitionSpec as P

PATCH = 128
F_DEV = 16
RIM = 3
LEAD = 8
LANES = 128


def split_bf16(values):
    high = values.astype(jnp.bfloat16)
    low = (values - high.astype(jnp.float32)).astype(jnp.bfloat16)
    return high, low


def dot(left, right):
    return jnp.dot(left, right, preferred_element_type=jnp.float32)


def brick_kernel(
    pieces_count, cx, cy, nt, patches, place,
    where_ref, low_ref, high_ref, band5_ref, band9_ref, faults_ref, *refs,
):
    pieces = refs[:pieces_count]
    picks_hbm, offsets_hbm, attr_hbm, partial_ref = refs[pieces_count:pieces_count + 4]
    amp, exy, ett, box, rows_bf, attr, picks, offsets, windows, sems = refs[pieces_count + 4:]
    halves = nt // LANES
    strip = cy // pieces_count
    brick, slab, bricks, slabs = where_ref[0], where_ref[1], where_ref[2], where_ref[3]
    wide = cy + 8

    fetches = []
    for d in range(pieces_count):
        column = pl.multiple_of(LEAD + strip * (brick ^ d), 8)
        for h in range(halves):
            fetches.append(pltpu.make_async_copy(
                pieces[d].at[:, :, pl.ds(h * LANES, LANES)],
                amp.at[:, h, pl.ds(column, strip), :],
                sems.at[d * halves + h],
            ))
    base = pieces_count * halves
    fetch_picks = pltpu.make_async_copy(picks_hbm, picks, sems.at[base])
    fetch_offsets = pltpu.make_async_copy(offsets_hbm, offsets, sems.at[base + 1])
    for copy in fetches:
        copy.start()
    fetch_picks.start()
    fetch_offsets.start()
    for h in range(halves):
        lanes = pl.ds(h * LANES, LANES)
        amp[:, h, LEAD - RIM:LEAD, :] = low_ref[:, :, lanes]
        amp[:, h, LEAD + cy:LEAD + cy + RIM, :] = high_ref[:, :, lanes]
    for copy in fetches:
        copy.wait()

    lane = lax.broadcasted_iota(jnp.int32, (wide, LANES), 1)
    first, last = lane == 0, lane == LANES - 1
    column = lax.broadcasted_iota(jnp.int32, (wide, LANES), 0)
    inside = jnp.logical_and(
        jnp.logical_or(slab > 0, column >= 2),
        jnp.logical_or(slab < slabs - 1, column < cy + 2),
    ).astype(jnp.float32)
    origin = LEAD - RIM

    def energy_row(e, carry):
        position = brick * cx + e - 2
        valid = jnp.logical_and(position >= 0, position < bricks * cx).astype(jnp.float32)
        mask = inside * valid
        centre = [amp[e + 1, h, origin + 1:origin + 1 + wide, :] for h in range(halves)]
        back = [pltpu.roll(c, 1, 1) for c in centre]
        ahead = [pltpu.roll(c, LANES - 1, 1) for c in centre]
        for h in range(halves):
            slope_x = (amp[e + 2, h, origin + 1:origin + 1 + wide, :]
                       - amp[e, h, origin + 1:origin + 1 + wide, :])
            slope_y = (amp[e + 1, h, origin + 2:origin + 2 + wide, :]
                       - amp[e + 1, h, origin:origin + wide, :])
            before = jnp.where(first, back[h - 1] if h > 0 else 0.0, back[h])
            after = jnp.where(last, ahead[h + 1] if h < halves - 1 else 0.0, ahead[h])
            slope_t = after - before
            exy[e, h] = (slope_x * slope_x + slope_y * slope_y) * mask
            ett[e, h] = slope_t * slope_t * mask
        return carry

    lax.fori_loop(0, cx + 4, energy_row, 0)

    def summed(field, slot, radius, rows, band):
        parts = []
        for h in range(halves):
            box[slot, h] = rows[h]
        for h in range(halves):
            total = box[slot, h, 0:cy, :]
            for j in range(1, 2 * radius + 1):
                total = total + box[slot, h, j:j + cy, :]
            parts.append(total)
        return parts

    def through_time(parts, band):
        whole = jnp.concatenate(parts, axis=1)
        high, low = split_bf16(whole)
        return dot(high, band) + dot(low, band)

    def attribute_row(r, carry):
        def inline5(field, h):
            total = field[r, h]
            for j in range(1, 5):
                total = total + field[r + j, h]
            return total

        tensor_xy = through_time(
            summed(exy, 0, 2, [inline5(exy, h) for h in range(halves)], None), band5_ref[...])
        tensor_t = through_time(
            summed(ett, 1, 2, [inline5(ett, h) for h in range(halves)], None), band5_ref[...])
        near = slice(LEAD - 1, LEAD - 1 + wide)
        stack_rows, power_rows = [], []
        for h in range(halves):
            rows = [amp[r + RIM + j, h, near, :] for j in (-1, 0, 1)]
            stack_rows.append(rows[0] + rows[1] + rows[2])
            power_rows.append(rows[0] * rows[0] + rows[1] * rows[1] + rows[2] * rows[2])
        stack = summed(None, 2, 1, stack_rows, None)
        power = summed(None, 3, 1, power_rows, None)
        spread = [9.0 * p - s * s for p, s in zip(power, stack)]
        scatter = through_time(spread, band9_ref[...]) + 1e-5
        whole = 9.0 * through_time(power, band9_ref[...]) + 1e-5
        both = whole * (tensor_xy + tensor_t + 4e-5)
        inverse = pl.reciprocal(both, approx=True)
        inverse = inverse * (2.0 - both * inverse)
        values = scatter * tensor_xy * inverse
        attr[r] = values
        high, low = split_bf16(values)
        at = pl.ds(pl.multiple_of(r * cy, 16), cy)
        rows_bf[at, 0:nt] = high
        rows_bf[at, nt:2 * nt] = low
        return carry

    lax.fori_loop(0, cx, attribute_row, 0)
    store = pltpu.make_async_copy(attr, attr_hbm, sems.at[base + 2])
    store.start()

    fetch_picks.wait()
    fetch_offsets.wait()
    block = 512
    lane_block = lax.broadcasted_iota(jnp.int32, (block, LANES), 1)

    def window_block(j, carry):
        at = pl.ds(pl.multiple_of(j * block, block), block)
        chosen = dot(picks[at, :], rows_bf[...])
        rows = chosen[:, 0:nt] + chosen[:, nt:2 * nt]
        shift = offsets[at, :]
        mixed = jnp.where(lane_block < shift, rows[:, LANES:nt], rows[:, 0:LANES])
        window = jnp.take_along_axis(mixed, (lane_block + shift) & (LANES - 1), axis=1)
        high, low = split_bf16(window)
        windows[at, 0:PATCH] = high
        windows[at, PATCH:2 * PATCH] = low
        return carry

    lax.fori_loop(0, patches // block, window_block, 0)
    sums = dot(faults_ref[...], windows[...])
    partial_ref[...] = sums[:, 0:PATCH] + sums[:, PATCH:2 * PATCH]
    store.wait()


def band(nt, radius):
    at = jnp.arange(nt, dtype=jnp.int32)
    return (jnp.abs(at[:, None] - at[None, :]) <= radius).astype(jnp.bfloat16)


def exchange_bricks(amp, cx):
    bricks = lax.axis_size("brick")
    mine = lax.axis_index("brick")
    padded = jnp.pad(amp, ((RIM, RIM), (0, 0), (0, 0)))
    pieces = []
    for d in range(bricks):
        piece = lax.dynamic_slice_in_dim(padded, (mine ^ d) * cx, cx + 2 * RIM, axis=0)
        if d > 0:
            piece = lax.ppermute(piece, "brick", [(s, s ^ d) for s in range(bricks)])
        pieces.append(piece)
    return pieces


def halo_columns(pieces, strip):
    bricks = lax.axis_size("brick")
    slabs = lax.axis_size("bulk")
    mine = lax.axis_index("brick")
    left = sum(jnp.where((mine ^ d) == 0, p[:, :RIM], 0.0) for d, p in enumerate(pieces))
    right = sum(
        jnp.where((mine ^ d) == bricks - 1, p[:, strip - RIM:], 0.0) for d, p in enumerate(pieces))
    low = lax.ppermute(right, "bulk", [(s, s + 1) for s in range(slabs - 1)])
    high = lax.ppermute(left, "bulk", [(s + 1, s) for s in range(slabs - 1)])
    return low, high


def reduce_scatter(parts, axis):
    count = lax.axis_size(axis)
    mine = lax.axis_index(axis)
    bit = 1
    while bit < count:
        pair = parts.reshape(parts.shape[0] // 2, 2, *parts.shape[1:])
        side = mine // bit % 2
        kept = lax.dynamic_index_in_dim(pair, side, 1, keepdims=False)
        sent = lax.dynamic_index_in_dim(pair, 1 - side, 1, keepdims=False)
        parts = kept + lax.ppermute(sent, axis, [(s, s ^ bit) for s in range(count)])
        bit *= 2
    return parts[0]


def local(amp_traces, patch_owner, patch_fault, patch_trace, patch_offset):
    bricks, slabs = lax.axis_size("brick"), lax.axis_size("bulk")
    nx, strip, nt = amp_traces.shape
    cx, cy = nx // bricks, strip * bricks
    patches = patch_fault.shape[0]
    faults = slabs * F_DEV

    pieces = exchange_bricks(amp_traces, cx)
    low, high = halo_columns(pieces, strip)

    picks = (patch_trace[:, None] == jnp.arange(cx * cy, dtype=jnp.int32)[None, :]).astype(jnp.bfloat16)
    offsets = jnp.broadcast_to(patch_offset[:, None], (patches, LANES))
    fault = patch_owner[:, 0] * F_DEV + patch_fault
    members = fault[None, :] == jnp.arange(faults, dtype=jnp.int32)[:, None]
    counts = jnp.sum(members.astype(jnp.float32), axis=1)
    members = members.astype(jnp.bfloat16)
    where = jnp.stack([
        lax.axis_index("brick"), lax.axis_index("bulk"), jnp.int32(bricks), jnp.int32(slabs)])

    halves = nt // LANES
    wide = cy + 8
    vmem = pl.BlockSpec(memory_space=pltpu.VMEM)
    anywhere = pl.BlockSpec(memory_space=pl.ANY)

    def kernel(*refs):
        brick_kernel(bricks, cx, cy, nt, patches, None, *refs)

    attribute, partial = pl.pallas_call(
        kernel,
        out_shape=(
            jax.ShapeDtypeStruct((cx, cy, nt), jnp.float32),
            jax.ShapeDtypeStruct((faults, PATCH), jnp.float32),
        ),
        in_specs=[pl.BlockSpec(memory_space=pltpu.SMEM)] + [vmem] * 5 + [anywhere] * (bricks + 2),
        out_specs=(anywhere, vmem),
        scratch_shapes=[
            pltpu.VMEM((cx + 2 * RIM, halves, cy + 2 * LEAD, LANES), jnp.float32),
            pltpu.VMEM((cx + 4, halves, wide, LANES), jnp.float32),
            pltpu.VMEM((cx + 4, halves, wide, LANES), jnp.float32),
            pltpu.VMEM((4, halves, wide, LANES), jnp.float32),
            pltpu.VMEM((cx * cy, 2 * nt), jnp.bfloat16),
            pltpu.VMEM((cx, cy, nt), jnp.float32),
            pltpu.VMEM((patches, cx * cy), jnp.bfloat16),
            pltpu.VMEM((patches, LANES), jnp.int32),
            pltpu.VMEM((patches, 2 * PATCH), jnp.bfloat16),
            pltpu.SemaphoreType.DMA((bricks * halves + 3,)),
        ],
        compiler_params=pltpu.CompilerParams(vmem_limit_bytes=48 * 1024 * 1024),
        cost_estimate=pl.CostEstimate(flops=2_500_000_000, bytes_accessed=10_000_000, transcendentals=0),
        name="brick_attribute",
    )(where, low, high, band(nt, 2), band(nt, 4), members, *pieces, picks, offsets)

    tally = jnp.pad(counts.reshape(slabs, 1, F_DEV), ((0, 0), (0, 0), (0, PATCH - F_DEV)))
    parts = jnp.concatenate([partial.reshape(slabs, F_DEV, PATCH), tally], axis=1)
    total = reduce_scatter(parts, "bulk")
    profile = total[:F_DEV] / jnp.maximum(total[F_DEV, :F_DEV], 1.0)[:, None]
    return attribute, profile


def solution(mesh):
    in_specs = (
        P(None, ("bulk", "brick"), None),
        P(("brick", "bulk"), None),
        P(("brick", "bulk")),
        P(("brick", "bulk")),
        P(("brick", "bulk")),
    )
    out_specs = (P("brick", "bulk", None), P(("brick", "bulk"), None))
    return jax.shard_map(local, mesh=mesh, in_specs=in_specs, out_specs=out_specs, check_vma=False)
```

```python
import jax
import jax.numpy as jnp
from jax import lax
from jax.experimental import pallas as pl
from jax.experimental.pallas import tpu as pltpu
from jax.sharding import PartitionSpec as P

PATCH = 128
F_DEV = 16
RIM = 3
LEAD = 8
LANES = 128
UNROLL_E = 5
UNROLL_S = 1
TILE_M = 1024
BLOCK = 1024


def split_bf16(values):
    high = values.astype(jnp.bfloat16)
    low = (values - high.astype(jnp.float32)).astype(jnp.bfloat16)
    return high, low


def dot(left, right):
    return jnp.dot(left, right, preferred_element_type=jnp.float32)


def brick_kernel(
    layout, strip, cx, cy, nt, patches,
    where_ref, low_ref, high_ref, band5_ref, band9_ref, faults_ref, *refs,
):
    pieces = refs[:len(layout)]
    picks_hbm, offsets_hbm, attr_hbm, partial_ref = refs[len(layout):len(layout) + 4]
    amp, exy, ett, box, fields, rows_bf, attr, picks, offsets, windows, sems = refs[len(layout) + 4:]
    halves = nt // LANES
    brick, slab, bricks, slabs = where_ref[0], where_ref[1], where_ref[2], where_ref[3]
    wide = cy + 8

    fetches = []
    for n, (d, part, width) in enumerate(layout):
        source = brick ^ d
        column = LEAD + strip * source + width * part_of(source, bricks, part)
        for h in range(halves):
            fetches.append(pltpu.make_async_copy(
                pieces[n].at[:, :, pl.ds(h * LANES, LANES)],
                amp.at[:, h, pl.ds(pl.multiple_of(column, 8), width), :],
                sems.at[n * halves + h],
            ))
    base = len(layout) * halves
    fetch_picks = pltpu.make_async_copy(picks_hbm, picks, sems.at[base])
    fetch_offsets = pltpu.make_async_copy(offsets_hbm, offsets, sems.at[base + 1])
    for copy in fetches:
        copy.start()
    fetch_picks.start()
    fetch_offsets.start()
    for h in range(halves):
        lanes = pl.ds(h * LANES, LANES)
        amp[:, h, LEAD - RIM:LEAD, :] = low_ref[:, :, lanes]
        amp[:, h, LEAD + cy:LEAD + cy + RIM, :] = high_ref[:, :, lanes]
    for copy in fetches:
        copy.wait()

    lane = lax.broadcasted_iota(jnp.int32, (wide, LANES), 1)
    first, last = lane == 0, lane == LANES - 1
    column = lax.broadcasted_iota(jnp.int32, (wide, LANES), 0)
    inside = jnp.logical_and(
        jnp.logical_or(slab > 0, column >= 2),
        jnp.logical_or(slab < slabs - 1, column < cy + 2),
    ).astype(jnp.float32)
    origin = LEAD - RIM

    def energy_row(e, carry):
        position = brick * cx + e - 2
        valid = jnp.logical_and(position >= 0, position < bricks * cx).astype(jnp.float32)
        mask = inside * valid
        centre = [amp[e + 1, h, origin + 1:origin + 1 + wide, :] for h in range(halves)]
        back = [pltpu.roll(c, 1, 1) for c in centre]
        ahead = [pltpu.roll(c, LANES - 1, 1) for c in centre]
        for h in range(halves):
            slope_x = (amp[e + 2, h, origin + 1:origin + 1 + wide, :]
                       - amp[e, h, origin + 1:origin + 1 + wide, :])
            slope_y = (amp[e + 1, h, origin + 2:origin + 2 + wide, :]
                       - amp[e + 1, h, origin:origin + wide, :])
            before = jnp.where(first, back[h - 1] if h > 0 else 0.0, back[h])
            after = jnp.where(last, ahead[h + 1] if h < halves - 1 else 0.0, ahead[h])
            slope_t = after - before
            exy[e, h] = (slope_x * slope_x + slope_y * slope_y) * mask
            ett[e, h] = slope_t * slope_t * mask
        return carry

    lax.fori_loop(0, cx + 4, energy_row, 0, unroll=UNROLL_E)

    def across(slot, h, radius, row):
        box[slot, h] = row
        total = box[slot, h, 0:cy, :]
        for j in range(1, 2 * radius + 1):
            total = total + box[slot, h, j:j + cy, :]
        return total

    def inline5(field, r, h):
        total = field[r, h]
        for j in range(1, 5):
            total = total + field[r + j, h]
        return total

    def keep(index, at, h, values):
        high, low = split_bf16(values)
        fields[index, 0, at, h * LANES:(h + 1) * LANES] = high
        fields[index, 1, at, h * LANES:(h + 1) * LANES] = low

    def sum_row(r, carry):
        at = pl.ds(pl.multiple_of(r * cy, 16), cy)
        near = slice(LEAD - 1, LEAD - 1 + wide)
        for h in range(halves):
            keep(0, at, h, across(0, h, 2, inline5(exy, r, h)))
            keep(1, at, h, across(1, h, 2, inline5(ett, r, h)))
            rows = [amp[r + RIM + j, h, near, :] for j in (-1, 0, 1)]
            stack = across(2, h, 1, rows[0] + rows[1] + rows[2])
            power = 9.0 * across(3, h, 1, rows[0] * rows[0] + rows[1] * rows[1] + rows[2] * rows[2])
            keep(2, at, h, power - stack * stack)
            keep(3, at, h, power)
        return carry

    lax.fori_loop(0, cx, sum_row, 0, unroll=UNROLL_S)

    band5, band9 = band5_ref[...], band9_ref[...]
    tile = TILE_M

    def finish_tile(j, carry):
        at = pl.ds(pl.multiple_of(j * tile, tile), tile)
        sums = [dot(fields[f, 0, at, :], b) + dot(fields[f, 1, at, :], b)
                for f, b in enumerate((band5, band5, band9, band9))]
        both = (sums[3] + 1e-5) * (sums[0] + sums[1] + 4e-5)
        inverse = pl.reciprocal(both, approx=True)
        inverse = inverse * (2.0 - both * inverse)
        values = (sums[2] + 1e-5) * sums[0] * inverse
        attr[at, :] = values
        high, low = split_bf16(values)
        rows_bf[at, 0:nt] = high
        rows_bf[at, nt:2 * nt] = low
        return carry

    lax.fori_loop(0, cx * cy // tile, finish_tile, 0)
    store = pltpu.make_async_copy(attr, attr_hbm, sems.at[base + 2])
    store.start()

    fetch_picks.wait()
    fetch_offsets.wait()
    block = BLOCK
    lane_block = lax.broadcasted_iota(jnp.int32, (block, LANES), 1)

    def window_block(j, carry):
        at = pl.ds(pl.multiple_of(j * block, block), block)
        chosen = dot(picks[at, :], rows_bf[...])
        rows = chosen[:, 0:nt] + chosen[:, nt:2 * nt]
        shift = offsets[at, :]
        mixed = jnp.where(lane_block < shift, rows[:, LANES:nt], rows[:, 0:LANES])
        window = jnp.take_along_axis(mixed, (lane_block + shift) & (LANES - 1), axis=1)
        high, low = split_bf16(window)
        windows[at, 0:PATCH] = high
        windows[at, PATCH:2 * PATCH] = low
        return carry

    lax.fori_loop(0, patches // block, window_block, 0)
    sums = dot(faults_ref[...], windows[...])
    partial_ref[...] = sums[:, 0:PATCH] + sums[:, PATCH:2 * PATCH]
    store.wait()


def band(nt, radius):
    at = jnp.arange(nt, dtype=jnp.int32)
    return (jnp.abs(at[:, None] - at[None, :]) <= radius).astype(jnp.bfloat16)


def part_of(strip_index, bricks, part):
    if part is None:
        return 0
    upper = (strip_index >= bricks // 2).astype(jnp.int32) if hasattr(strip_index, "astype") else int(
        strip_index >= bricks // 2)
    return upper if part == 0 else 1 - upper


def exchange_bricks(amp, cx):
    bricks = lax.axis_size("brick")
    mine = lax.axis_index("brick")
    strip = amp.shape[1]
    padded = jnp.pad(amp, ((RIM, RIM), (0, 0), (0, 0)))
    rows = cx + 2 * RIM
    parts, width = ((0, 1), strip // 2) if strip % 16 == 0 else ((None,), strip)
    pieces, layout = [], []
    for part in parts:
        begin = width * part_of(mine, bricks, part)
        for d in range(1, bricks):
            piece = lax.dynamic_slice(
                padded, ((mine ^ d) * cx, begin, 0), (rows, width, amp.shape[2]))
            pieces.append(lax.ppermute(piece, "brick", [(s, s ^ d) for s in range(bricks)]))
            layout.append((d, part, width))
    pieces.append(lax.dynamic_slice_in_dim(padded, mine * cx, rows, axis=0))
    layout.append((0, None, strip))
    return pieces, layout


def halo_columns(pieces, layout):
    bricks = lax.axis_size("brick")
    slabs = lax.axis_size("bulk")
    mine = lax.axis_index("brick")
    left, right = 0.0, 0.0
    for piece, (d, part, width) in zip(pieces, layout):
        if part != 1:
            left = jnp.where((mine ^ d) == 0, piece[:, :RIM], left)
            right = jnp.where((mine ^ d) == bricks - 1, piece[:, width - RIM:], right)
    low = lax.ppermute(right, "bulk", [(s, s + 1) for s in range(slabs - 1)])
    high = lax.ppermute(left, "bulk", [(s + 1, s) for s in range(slabs - 1)])
    return low, high


def reduce_scatter(parts, axis):
    count = lax.axis_size(axis)
    mine = lax.axis_index(axis)
    bit = 1
    while bit < count:
        pair = parts.reshape(parts.shape[0] // 2, 2, *parts.shape[1:])
        side = mine // bit % 2
        kept = lax.dynamic_index_in_dim(pair, side, 1, keepdims=False)
        sent = lax.dynamic_index_in_dim(pair, 1 - side, 1, keepdims=False)
        parts = kept + lax.ppermute(sent, axis, [(s, s ^ bit) for s in range(count)])
        bit *= 2
    return parts[0]


def local(amp_traces, patch_owner, patch_fault, patch_trace, patch_offset):
    bricks, slabs = lax.axis_size("brick"), lax.axis_size("bulk")
    nx, strip, nt = amp_traces.shape
    cx, cy = nx // bricks, strip * bricks
    patches = patch_fault.shape[0]
    faults = slabs * F_DEV

    pieces, layout = exchange_bricks(amp_traces, cx)
    low, high = halo_columns(pieces, layout)

    picks = (patch_trace[:, None] == jnp.arange(cx * cy, dtype=jnp.int32)[None, :]).astype(jnp.bfloat16)
    offsets = jnp.broadcast_to(patch_offset[:, None], (patches, LANES))
    fault = patch_owner[:, 0] * F_DEV + patch_fault
    members = fault[None, :] == jnp.arange(faults, dtype=jnp.int32)[:, None]
    counts = jnp.sum(members.astype(jnp.float32), axis=1)
    members = members.astype(jnp.bfloat16)
    where = jnp.stack([
        lax.axis_index("brick"), lax.axis_index("bulk"), jnp.int32(bricks), jnp.int32(slabs)])

    halves = nt // LANES
    wide = cy + 8
    vmem = pl.BlockSpec(memory_space=pltpu.VMEM)
    anywhere = pl.BlockSpec(memory_space=pl.ANY)

    def kernel(*refs):
        brick_kernel(layout, strip, cx, cy, nt, patches, *refs)

    attribute, partial = pl.pallas_call(
        kernel,
        out_shape=(
            jax.ShapeDtypeStruct((cx * cy, nt), jnp.float32),
            jax.ShapeDtypeStruct((faults, PATCH), jnp.float32),
        ),
        in_specs=[pl.BlockSpec(memory_space=pltpu.SMEM)] + [vmem] * 5 + [anywhere] * (len(layout) + 2),
        out_specs=(anywhere, vmem),
        scratch_shapes=[
            pltpu.VMEM((cx + 2 * RIM, halves, cy + 2 * LEAD, LANES), jnp.float32),
            pltpu.VMEM((cx + 4, halves, wide, LANES), jnp.float32),
            pltpu.VMEM((cx + 4, halves, wide, LANES), jnp.float32),
            pltpu.VMEM((4, halves, wide, LANES), jnp.float32),
            pltpu.VMEM((4, 2, cx * cy, nt), jnp.bfloat16),
            pltpu.VMEM((cx * cy, 2 * nt), jnp.bfloat16),
            pltpu.VMEM((cx * cy, nt), jnp.float32),
            pltpu.VMEM((patches, cx * cy), jnp.bfloat16),
            pltpu.VMEM((patches, LANES), jnp.int32),
            pltpu.VMEM((patches, 2 * PATCH), jnp.bfloat16),
            pltpu.SemaphoreType.DMA((len(layout) * halves + 3,)),
        ],
        compiler_params=pltpu.CompilerParams(vmem_limit_bytes=48 * 1024 * 1024),
        cost_estimate=pl.CostEstimate(flops=2_500_000_000, bytes_accessed=10_000_000, transcendentals=0),
        name="brick_attribute",
    )(where, low, high, band(nt, 2), band(nt, 4), members, *pieces, picks, offsets)

    tally = jnp.pad(counts.reshape(slabs, 1, F_DEV), ((0, 0), (0, 0), (0, PATCH - F_DEV)))
    parts = jnp.concatenate([partial.reshape(slabs, F_DEV, PATCH), tally], axis=1)
    total = reduce_scatter(parts, "bulk")
    profile = total[:F_DEV] / jnp.maximum(total[F_DEV, :F_DEV], 1.0)[:, None]
    return attribute.reshape(cx, cy, nt), profile


def solution(mesh):
    in_specs = (
        P(None, ("bulk", "brick"), None),
        P(("brick", "bulk"), None),
        P(("brick", "bulk")),
        P(("brick", "bulk")),
        P(("brick", "bulk")),
    )
    out_specs = (P("brick", "bulk", None), P(("brick", "bulk"), None))
    return jax.shard_map(local, mesh=mesh, in_specs=in_specs, out_specs=out_specs, check_vma=False)
```

```python
import jax
import jax.numpy as jnp
from jax import lax
from jax.experimental import pallas as pl
from jax.experimental.pallas import tpu as pltpu
from jax.sharding import PartitionSpec as P

PATCH = 128
F_DEV = 16
RIM = 3
LEAD = 8
LANES = 128
TILE_M = 1024
BLOCK = 256


def split_bf16(values):
    high = values.astype(jnp.bfloat16)
    low = (values - high.astype(jnp.float32)).astype(jnp.bfloat16)
    return high, low


def dot(left, right):
    return jnp.dot(left, right, preferred_element_type=jnp.float32)


def brick_kernel(
    layout, strip, cx, cy, nt, patches,
    where_ref, low_ref, high_ref, band5_ref, band9_ref, faults_ref, *refs,
):
    pieces = refs[:len(layout)]
    picks_hbm, offsets_hbm, attr_hbm, partial_ref = refs[len(layout):len(layout) + 4]
    amp, exy, ett, box, fields, rows_bf, attr, picks, offsets, windows, sems = refs[len(layout) + 4:]
    halves = nt // LANES
    brick, slab, bricks, slabs = where_ref[0], where_ref[1], where_ref[2], where_ref[3]
    wide = cy + 8

    rows = cx + 2 * RIM
    top = jnp.where(brick == 0, 2 * RIM, jnp.where(brick == bricks - 1, 0, RIM))
    fetches = []
    for n, (d, part, width) in enumerate(layout):
        source = brick ^ d
        column = LEAD + strip * source + width * part_of(source, bricks, part)
        piece = pieces[n] if d else pieces[n].at[pl.ds(brick * cx + top - 2 * RIM, rows)]
        for h in range(halves):
            fetches.append(pltpu.make_async_copy(
                piece.at[:, :, pl.ds(h * LANES, LANES)],
                amp.at[h, pl.ds(top, rows), pl.ds(pl.multiple_of(column, 8), width), :],
                sems.at[n * halves + h],
            ))
    base = len(layout) * halves
    fetch_picks = pltpu.make_async_copy(picks_hbm, picks, sems.at[base])
    fetch_offsets = pltpu.make_async_copy(offsets_hbm, offsets, sems.at[base + 1])
    for copy in fetches:
        copy.start()
    fetch_picks.start()
    fetch_offsets.start()
    even = lax.rem(slab, 2) == 0
    for h in range(halves):
        lanes = pl.ds(h * LANES, LANES)
        near, far = low_ref[:, :, lanes], high_ref[:, :, lanes]
        amp[h, pl.ds(top, rows), LEAD - RIM:LEAD, :] = jnp.where(even, far, near)
        amp[h, pl.ds(top, rows), LEAD + cy:LEAD + cy + RIM, :] = jnp.where(even, near, far)
    for copy in fetches:
        copy.wait()

    @pl.when(brick == 0)
    def _():
        amp[:, RIM:2 * RIM] = jnp.zeros((halves, RIM) + amp.shape[2:], jnp.float32)

    @pl.when(brick == bricks - 1)
    def _():
        amp[:, cx + 2 * RIM:cx + 3 * RIM] = jnp.zeros((halves, RIM) + amp.shape[2:], jnp.float32)

    lane = lax.broadcasted_iota(jnp.int32, (wide, LANES), 1)
    first, last = lane == 0, lane == LANES - 1
    column = lax.broadcasted_iota(jnp.int32, (wide, LANES), 0)
    inside = jnp.logical_and(
        jnp.logical_or(slab > 0, column >= 2),
        jnp.logical_or(slab < slabs - 1, column < cy + 2),
    ).astype(jnp.float32)
    origin = LEAD - RIM

    def energy_row(e, carry):
        position = brick * cx + e - 2
        valid = jnp.logical_and(position >= 0, position < bricks * cx).astype(jnp.float32)
        mask = inside * valid
        centre = [amp[h, e + 1 + RIM, origin + 1:origin + 1 + wide, :] for h in range(halves)]
        back = [pltpu.roll(c, 1, 1) for c in centre]
        ahead = [pltpu.roll(c, LANES - 1, 1) for c in centre]
        for h in range(halves):
            slope_x = (amp[h, e + 2 + RIM, origin + 1:origin + 1 + wide, :]
                       - amp[h, e + RIM, origin + 1:origin + 1 + wide, :])
            slope_y = (amp[h, e + 1 + RIM, origin + 2:origin + 2 + wide, :]
                       - amp[h, e + 1 + RIM, origin:origin + wide, :])
            before = jnp.where(first, back[h - 1] if h > 0 else 0.0, back[h])
            after = jnp.where(last, ahead[h + 1] if h < halves - 1 else 0.0, ahead[h])
            slope_t = after - before
            exy[e, h] = (slope_x * slope_x + slope_y * slope_y) * mask
            ett[e, h] = slope_t * slope_t * mask
        return carry

    lax.fori_loop(0, cx + 4, energy_row, 0, unroll=True)

    def across(slot, h, radius, row):
        box[slot, h] = row
        total = box[slot, h, 0:cy, :]
        for j in range(1, 2 * radius + 1):
            total = total + box[slot, h, j:j + cy, :]
        return total

    def inline5(field, r, h):
        e = [field[r + j, h] for j in range(8)]
        low, middle, high = e[1] + e[2], e[3] + e[4], e[5] + e[6]
        left, right = low + middle, middle + high
        return left + e[0], left + e[5], right + e[2], right + e[7]

    def inline3(e):
        low, high = e[1] + e[2], e[3] + e[4]
        return low + e[0], low + e[3], high + e[2], high + e[5]

    def keep(index, at, h, values):
        high, low = split_bf16(values)
        fields[index, 0, at, h * LANES:(h + 1) * LANES] = high
        fields[index, 1, at, h * LANES:(h + 1) * LANES] = low

    def sum_rows(q, carry):
        r = 4 * q
        near = slice(LEAD - 1, LEAD - 1 + wide)
        for h in range(halves):
            rows = [amp[h, r + 2 * RIM - 1 + j, near, :] for j in range(6)]
            stacks = inline3(rows)
            powers = inline3([row * row for row in rows])
            xys, ts = inline5(exy, r, h), inline5(ett, r, h)
            for j in range(4):
                at = pl.ds(pl.multiple_of((r + j) * cy, 16), cy)
                keep(0, at, h, across(4 * j + 0, h, 2, xys[j]))
                keep(1, at, h, across(4 * j + 1, h, 2, ts[j]))
                stack = across(4 * j + 2, h, 1, stacks[j])
                power = 9.0 * across(4 * j + 3, h, 1, powers[j])
                keep(2, at, h, power - stack * stack)
                keep(3, at, h, power)
        return carry

    lax.fori_loop(0, cx // 4, sum_rows, 0, unroll=True)

    band5, band9 = band5_ref[...], band9_ref[...]
    tile = TILE_M

    def finish_tile(j, carry):
        at = pl.ds(pl.multiple_of(j * tile, tile), tile)
        sums = [dot(fields[f, 0, at, :], b) + dot(fields[f, 1, at, :], b)
                for f, b in enumerate((band5, band5, band9, band9))]
        both = (sums[3] + 1e-5) * (sums[0] + sums[1] + 4e-5)
        inverse = pl.reciprocal(both, approx=True)
        inverse = inverse * (2.0 - both * inverse)
        values = (sums[2] + 1e-5) * sums[0] * inverse
        attr[at, :] = values
        high, low = split_bf16(values)
        rows_bf[at, 0:nt] = high
        rows_bf[at, nt:2 * nt] = low
        return carry

    lax.fori_loop(0, cx * cy // tile, finish_tile, 0)
    store = pltpu.make_async_copy(attr, attr_hbm, sems.at[base + 2])
    store.start()

    fetch_picks.wait()
    fetch_offsets.wait()
    block = BLOCK
    lane_block = lax.broadcasted_iota(jnp.int32, (block, LANES), 1)

    def window_block(j, carry):
        at = pl.ds(pl.multiple_of(j * block, block), block)
        chosen = dot(picks[at, :], rows_bf[...])
        rows = chosen[:, 0:nt] + chosen[:, nt:2 * nt]
        shift = offsets[at, :]
        mixed = jnp.where(lane_block < shift, rows[:, LANES:nt], rows[:, 0:LANES])
        window = jnp.take_along_axis(mixed, (lane_block + shift) & (LANES - 1), axis=1)
        high, low = split_bf16(window)
        windows[at, 0:PATCH] = high
        windows[at, PATCH:2 * PATCH] = low
        return carry

    lax.fori_loop(0, patches // block, window_block, 0, unroll=True)
    sums = dot(faults_ref[...], windows[...])
    partial_ref[...] = sums[:, 0:PATCH] + sums[:, PATCH:2 * PATCH]
    store.wait()


def band(nt, radius):
    at = jnp.arange(nt, dtype=jnp.int32)
    return (jnp.abs(at[:, None] - at[None, :]) <= radius).astype(jnp.bfloat16)


def part_of(strip_index, bricks, part):
    if part is None:
        return 0
    upper = (strip_index >= bricks // 2).astype(jnp.int32) if hasattr(strip_index, "astype") else int(
        strip_index >= bricks // 2)
    return upper if part == 0 else 1 - upper


def exchange_bricks(amp, cx):
    bricks = lax.axis_size("brick")
    mine = lax.axis_index("brick")
    nx, strip, nt = amp.shape
    rows = cx + 2 * RIM
    parts, width = ((0, 1), strip // 2) if strip % 16 == 0 else ((None,), strip)
    order = (bricks - 1, *range(1, bricks - 1))
    pieces, layout = [], []

    def cut(source, d, begin, columns):
        first = jnp.clip((mine ^ d) * cx - RIM, 0, nx - rows)
        return lax.dynamic_slice(source, (first, begin, 0), (rows, columns, nt))

    def send(piece, d):
        return lax.ppermute(piece, "brick", [(s, s ^ d) for s in range(bricks)])

    source = amp
    for part in parts:
        begin = width * part_of(mine, bricks, part)
        for n, d in enumerate(order):
            piece = cut(source, d, begin, width)
            if part == 1:
                piece, _ = lax.optimization_barrier((piece, pieces[n]))
            elif n == 0:
                source, piece = lax.optimization_barrier((amp, piece))
            pieces.append(send(piece, d))
            layout.append((d, part, width))
    pieces.append(amp)
    layout.append((0, None, strip))
    return pieces, layout


def halo_columns(pieces, layout, cx, prepared):
    bricks = lax.axis_size("brick")
    slabs = lax.axis_size("bulk")
    mine = lax.axis_index("brick")
    rows = cx + 2 * RIM
    left, right = 0.0, 0.0
    for piece, (d, part, width) in zip(pieces, layout):
        if d == 0:
            first = jnp.clip(mine * cx - RIM, 0, piece.shape[0] - rows)
            piece = lax.dynamic_slice_in_dim(piece, first, rows, axis=0)
        if part != 1:
            left = jnp.where((mine ^ d) == 0, piece[:, :RIM], left)
            right = jnp.where((mine ^ d) == bricks - 1, piece[:, width - RIM:], right)
    left, right, *prepared = lax.optimization_barrier((left, right, *prepared))
    even = lax.axis_index("bulk") % 2 == 0
    inner = [p for s in range(0, slabs - 1, 2) for p in ((s, s + 1), (s + 1, s))]
    outer = [p for s in range(1, slabs - 1, 2) for p in ((s, s + 1), (s + 1, s))]
    near, far = jnp.where(even, right, left), jnp.where(even, left, right)
    far = lax.ppermute(far, "bulk", outer)
    near = lax.ppermute(near, "bulk", inner)
    low, high = near, far
    return low, high, prepared


def reduce_scatter(parts, axis):
    count = lax.axis_size(axis)
    mine = lax.axis_index(axis)
    bit = 1
    while bit < count:
        pair = parts.reshape(parts.shape[0] // 2, 2, *parts.shape[1:])
        side = mine // bit % 2
        kept = lax.dynamic_index_in_dim(pair, side, 1, keepdims=False)
        sent = lax.dynamic_index_in_dim(pair, 1 - side, 1, keepdims=False)
        parts = kept + lax.ppermute(sent, axis, [(s, s ^ bit) for s in range(count)])
        bit *= 2
    return parts[0]


def local(amp_traces, patch_owner, patch_fault, patch_trace, patch_offset):
    bricks, slabs = lax.axis_size("brick"), lax.axis_size("bulk")
    nx, strip, nt = amp_traces.shape
    cx, cy = nx // bricks, strip * bricks
    patches = patch_fault.shape[0]
    faults = slabs * F_DEV

    pieces, layout = exchange_bricks(amp_traces, cx)
    offsets = jnp.broadcast_to(patch_offset[:, None], (patches, LANES))
    low, high, (offsets,) = halo_columns(pieces, layout, cx, (offsets,))

    picks = (patch_trace[:, None] == jnp.arange(cx * cy, dtype=jnp.int32)[None, :]).astype(jnp.bfloat16)
    fault = patch_owner[:, 0] * F_DEV + patch_fault
    members = fault[None, :] == jnp.arange(faults, dtype=jnp.int32)[:, None]
    counts = jnp.sum(members.astype(jnp.float32), axis=1)
    members = members.astype(jnp.bfloat16)
    where = jnp.stack([
        lax.axis_index("brick"), lax.axis_index("bulk"), jnp.int32(bricks), jnp.int32(slabs)])

    halves = nt // LANES
    wide = cy + 8
    vmem = pl.BlockSpec(memory_space=pltpu.VMEM)
    anywhere = pl.BlockSpec(memory_space=pl.ANY)

    def kernel(*refs):
        brick_kernel(layout, strip, cx, cy, nt, patches, *refs)

    attribute, partial = pl.pallas_call(
        kernel,
        out_shape=(
            jax.ShapeDtypeStruct((cx * cy, nt), jnp.float32),
            jax.ShapeDtypeStruct((faults, PATCH), jnp.float32),
        ),
        in_specs=[pl.BlockSpec(memory_space=pltpu.SMEM)] + [vmem] * 5 + [anywhere] * (len(layout) + 2),
        out_specs=(anywhere, vmem),
        scratch_shapes=[
            pltpu.VMEM((halves, cx + 4 * RIM, cy + 2 * LEAD, LANES), jnp.float32),
            pltpu.VMEM((cx + 4, halves, wide, LANES), jnp.float32),
            pltpu.VMEM((cx + 4, halves, wide, LANES), jnp.float32),
            pltpu.VMEM((16, halves, wide, LANES), jnp.float32),
            pltpu.VMEM((4, 2, cx * cy, nt), jnp.bfloat16),
            pltpu.VMEM((cx * cy, 2 * nt), jnp.bfloat16),
            pltpu.VMEM((cx * cy, nt), jnp.float32),
            pltpu.VMEM((patches, cx * cy), jnp.bfloat16),
            pltpu.VMEM((patches, LANES), jnp.int32),
            pltpu.VMEM((patches, 2 * PATCH), jnp.bfloat16),
            pltpu.SemaphoreType.DMA((len(layout) * halves + 3,)),
        ],
        compiler_params=pltpu.CompilerParams(vmem_limit_bytes=48 * 1024 * 1024),
        cost_estimate=pl.CostEstimate(flops=2_500_000_000, bytes_accessed=10_000_000, transcendentals=0),
        name="brick_attribute",
    )(where, low, high, band(nt, 2), band(nt, 4), members, *pieces, picks, offsets)

    tally = jnp.pad(counts.reshape(slabs, 1, F_DEV), ((0, 0), (0, 0), (0, PATCH - F_DEV)))
    parts = jnp.concatenate([partial.reshape(slabs, F_DEV, PATCH), tally], axis=1)
    total = reduce_scatter(parts, "bulk")
    profile = total[:F_DEV] / jnp.maximum(total[F_DEV, :F_DEV], 1.0)[:, None]
    return attribute.reshape(cx, cy, nt), profile


def solution(mesh):
    in_specs = (
        P(None, ("bulk", "brick"), None),
        P(("brick", "bulk"), None),
        P(("brick", "bulk")),
        P(("brick", "bulk")),
        P(("brick", "bulk")),
    )
    out_specs = (P("brick", "bulk", None), P(("brick", "bulk"), None))
    return jax.shard_map(local, mesh=mesh, in_specs=in_specs, out_specs=out_specs, check_vma=False)
```

```python
import jax
import jax.numpy as jnp
from jax import lax
from jax.experimental import pallas as pl
from jax.experimental.pallas import tpu as pltpu
from jax.sharding import PartitionSpec as P

PATCH = 128
F_DEV = 16
RIM = 3
LEAD = 8
LANES = 128
TIES = (0, 0, 0)
WHICH = 2
TILE_M = 1024
BLOCK = 256


def split_bf16(values):
    high = values.astype(jnp.bfloat16)
    low = (values - high.astype(jnp.float32)).astype(jnp.bfloat16)
    return high, low


def dot(left, right):
    return jnp.dot(left, right, preferred_element_type=jnp.float32)


def brick_kernel(
    layout, strip, cx, cy, nt, patches,
    where_ref, low_ref, high_ref, band5_ref, band9_ref, faults_ref, *refs,
):
    pieces = refs[:len(layout)]
    places_hbm, attr_hbm, partial_ref = refs[len(layout):len(layout) + 3]
    amp, exy, ett, box, fields, rows_bf, attr, places, windows, sems = refs[len(layout) + 3:]
    halves = nt // LANES
    brick, slab, bricks, slabs = where_ref[0], where_ref[1], where_ref[2], where_ref[3]
    wide = cy + 8

    rows = cx + 2 * RIM
    top = jnp.where(brick == 0, 2 * RIM, jnp.where(brick == bricks - 1, 0, RIM))
    fetches = []
    for n, (d, part, width) in enumerate(layout):
        source = brick ^ d
        column = LEAD + strip * source + width * part_of(source, bricks, part)
        piece = pieces[n] if d else pieces[n].at[pl.ds(brick * cx + top - 2 * RIM, rows)]
        for h in range(halves):
            fetches.append(pltpu.make_async_copy(
                piece.at[:, :, pl.ds(h * LANES, LANES)],
                amp.at[h, pl.ds(top, rows), pl.ds(pl.multiple_of(column, 8), width), :],
                sems.at[n * halves + h],
            ))
    base = len(layout) * halves
    fetch_places = pltpu.make_async_copy(places_hbm, places, sems.at[base])
    for copy in fetches:
        copy.start()
    fetch_places.start()
    even = lax.rem(slab, 2) == 0
    for h in range(halves):
        lanes = pl.ds(h * LANES, LANES)
        near, far = low_ref[:, :, lanes], high_ref[:, :, lanes]
        amp[h, pl.ds(top, rows), LEAD - RIM:LEAD, :] = jnp.where(even, far, near)
        amp[h, pl.ds(top, rows), LEAD + cy:LEAD + cy + RIM, :] = jnp.where(even, near, far)
    for copy in fetches:
        copy.wait()

    @pl.when(brick == 0)
    def _():
        amp[:, RIM:2 * RIM] = jnp.zeros((halves, RIM) + amp.shape[2:], jnp.float32)

    @pl.when(brick == bricks - 1)
    def _():
        amp[:, cx + 2 * RIM:cx + 3 * RIM] = jnp.zeros((halves, RIM) + amp.shape[2:], jnp.float32)

    lane = lax.broadcasted_iota(jnp.int32, (wide, LANES), 1)
    first, last = lane == 0, lane == LANES - 1
    column = lax.broadcasted_iota(jnp.int32, (wide, LANES), 0)
    inside = jnp.logical_and(
        jnp.logical_or(slab > 0, column >= 2),
        jnp.logical_or(slab < slabs - 1, column < cy + 2),
    ).astype(jnp.float32)
    origin = LEAD - RIM

    def energy_row(e, carry):
        position = brick * cx + e - 2
        valid = jnp.logical_and(position >= 0, position < bricks * cx).astype(jnp.float32)
        mask = inside * valid
        centre = [amp[h, e + 1 + RIM, origin + 1:origin + 1 + wide, :] for h in range(halves)]
        back = [pltpu.roll(c, 1, 1) for c in centre]
        ahead = [pltpu.roll(c, LANES - 1, 1) for c in centre]
        for h in range(halves):
            slope_x = (amp[h, e + 2 + RIM, origin + 1:origin + 1 + wide, :]
                       - amp[h, e + RIM, origin + 1:origin + 1 + wide, :])
            slope_y = (amp[h, e + 1 + RIM, origin + 2:origin + 2 + wide, :]
                       - amp[h, e + 1 + RIM, origin:origin + wide, :])
            before = jnp.where(first, back[h - 1] if h > 0 else 0.0, back[h])
            after = jnp.where(last, ahead[h + 1] if h < halves - 1 else 0.0, ahead[h])
            slope_t = after - before
            exy[e, h] = (slope_x * slope_x + slope_y * slope_y) * mask
            ett[e, h] = slope_t * slope_t * mask
        return carry

    lax.fori_loop(0, cx + 4, energy_row, 0, unroll=True)

    def across(slot, h, radius, row):
        box[slot, h] = row
        total = box[slot, h, 0:cy, :]
        for j in range(1, 2 * radius + 1):
            total = total + box[slot, h, j:j + cy, :]
        return total

    def inline5(field, r, h):
        e = [field[r + j, h] for j in range(8)]
        low, middle, high = e[1] + e[2], e[3] + e[4], e[5] + e[6]
        left, right = low + middle, middle + high
        return left + e[0], left + e[5], right + e[2], right + e[7]

    def inline3(e):
        low, high = e[1] + e[2], e[3] + e[4]
        return low + e[0], low + e[3], high + e[2], high + e[5]

    def keep(index, at, h, values):
        high, low = split_bf16(values)
        fields[index, 0, at, h * LANES:(h + 1) * LANES] = high
        fields[index, 1, at, h * LANES:(h + 1) * LANES] = low

    def sum_rows(q, carry):
        r = 4 * q
        near = slice(LEAD - 1, LEAD - 1 + wide)
        for h in range(halves):
            rows = [amp[h, r + 2 * RIM - 1 + j, near, :] for j in range(6)]
            stacks = inline3(rows)
            powers = inline3([row * row for row in rows])
            xys, ts = inline5(exy, r, h), inline5(ett, r, h)
            for j in range(4):
                at = pl.ds(pl.multiple_of((r + j) * cy, 16), cy)
                keep(0, at, h, across(4 * j + 0, h, 2, xys[j]))
                keep(1, at, h, across(4 * j + 1, h, 2, ts[j]))
                stack = across(4 * j + 2, h, 1, stacks[j])
                power = 9.0 * across(4 * j + 3, h, 1, powers[j])
                keep(2, at, h, power - stack * stack)
                keep(3, at, h, power)
        return carry

    lax.fori_loop(0, cx // 4, sum_rows, 0, unroll=True)

    band5, band9 = band5_ref[...], band9_ref[...]
    tile = TILE_M

    def finish_tile(j, carry):
        at = pl.ds(pl.multiple_of(j * tile, tile), tile)
        sums = [dot(fields[f, 0, at, :], b) + dot(fields[f, 1, at, :], b)
                for f, b in enumerate((band5, band5, band9, band9))]
        both = (sums[3] + 1e-5) * (sums[0] + sums[1] + 4e-5)
        inverse = pl.reciprocal(both, approx=True)
        inverse = inverse * (2.0 - both * inverse)
        values = (sums[2] + 1e-5) * sums[0] * inverse
        attr[at, :] = values
        high, low = split_bf16(values)
        rows_bf[at, 0:nt] = high
        rows_bf[at, nt:2 * nt] = low
        return carry

    lax.fori_loop(0, cx * cy // tile, finish_tile, 0)
    store = pltpu.make_async_copy(attr, attr_hbm, sems.at[base + 1])
    store.start()

    fetch_places.wait()
    block = BLOCK
    lane_block = lax.broadcasted_iota(jnp.int32, (block, LANES), 1)

    def window_block(j, carry):
        at = pl.ds(pl.multiple_of(j * block, block), block)
        place = places[at, :]
        trace = lax.shift_right_logical(place, nt.bit_length() - 1)
        chosen = dot(jnp.concatenate([
            (lane_block + k == trace).astype(jnp.float32).astype(jnp.bfloat16)
            for k in range(0, cx * cy, LANES)], axis=1), rows_bf[...])
        rows = chosen[:, 0:nt] + chosen[:, nt:2 * nt]
        shift = place - trace * nt
        mixed = jnp.where(lane_block < shift, rows[:, LANES:nt], rows[:, 0:LANES])
        window = jnp.take_along_axis(mixed, (lane_block + shift) & (LANES - 1), axis=1)
        high, low = split_bf16(window)
        windows[at, 0:PATCH] = high
        windows[at, PATCH:2 * PATCH] = low
        return carry

    lax.fori_loop(0, patches // block, window_block, 0, unroll=True)
    sums = dot(faults_ref[...], windows[...])
    partial_ref[...] = sums[:, 0:PATCH] + sums[:, PATCH:2 * PATCH]
    store.wait()


def band(nt, radius):
    at = jnp.arange(nt, dtype=jnp.int32)
    return (jnp.abs(at[:, None] - at[None, :]) <= radius).astype(jnp.bfloat16)


def part_of(strip_index, bricks, part):
    if part is None:
        return 0
    upper = (strip_index >= bricks // 2).astype(jnp.int32) if hasattr(strip_index, "astype") else int(
        strip_index >= bricks // 2)
    return upper if part == 0 else 1 - upper


def exchange_bricks(amp, cx, prepared):
    bricks = lax.axis_size("brick")
    mine = lax.axis_index("brick")
    nx, strip, nt = amp.shape
    rows = cx + 2 * RIM
    parts, width = ((0, 1), strip // 2) if strip % 16 == 0 else ((None,), strip)
    order = (bricks - 1, *range(1, bricks - 1))
    pieces, layout = [], []

    def cut(source, d, begin, columns):
        first = jnp.clip((mine ^ d) * cx - RIM, 0, nx - rows)
        return lax.dynamic_slice(source, (first, begin, 0), (rows, columns, nt))

    def send(piece, d):
        return lax.ppermute(piece, "brick", [(s, s ^ d) for s in range(bricks)])

    source = amp
    for part in parts:
        begin = width * part_of(mine, bricks, part)
        for n, d in enumerate(order):
            piece = cut(source, d, begin, width)
            if part == 1:
                if n == WHICH:
                    piece, _, prepared = lax.optimization_barrier((piece, pieces[TIES[n]], prepared))
                else:
                    piece, _ = lax.optimization_barrier((piece, pieces[TIES[n]]))
            elif n == 0:
                source, piece = lax.optimization_barrier((amp, piece))
            pieces.append(send(piece, d))
            layout.append((d, part, width))
    pieces.append(amp)
    layout.append((0, None, strip))
    return pieces, layout, prepared


def halo_columns(pieces, layout, cx, prepared):
    bricks = lax.axis_size("brick")
    slabs = lax.axis_size("bulk")
    mine = lax.axis_index("brick")
    rows = cx + 2 * RIM
    left, right = 0.0, 0.0
    for piece, (d, part, width) in zip(pieces, layout):
        if d == 0:
            first = jnp.clip(mine * cx - RIM, 0, piece.shape[0] - rows)
            piece = lax.dynamic_slice_in_dim(piece, first, rows, axis=0)
        if part != 1:
            left = jnp.where((mine ^ d) == 0, piece[:, :RIM], left)
            right = jnp.where((mine ^ d) == bricks - 1, piece[:, width - RIM:], right)
    left, right, *prepared = lax.optimization_barrier((left, right, *prepared))
    even = lax.axis_index("bulk") % 2 == 0
    inner = [p for s in range(0, slabs - 1, 2) for p in ((s, s + 1), (s + 1, s))]
    outer = [p for s in range(1, slabs - 1, 2) for p in ((s, s + 1), (s + 1, s))]
    near, far = jnp.where(even, right, left), jnp.where(even, left, right)
    far = lax.ppermute(far, "bulk", outer)
    near = lax.ppermute(near, "bulk", inner)
    low, high = near, far
    return low, high, prepared


def reduce_scatter(parts, axis):
    count = lax.axis_size(axis)
    mine = lax.axis_index(axis)
    bit = 1
    while bit < count:
        pair = parts.reshape(parts.shape[0] // 2, 2, *parts.shape[1:])
        side = mine // bit % 2
        kept = lax.dynamic_index_in_dim(pair, side, 1, keepdims=False)
        sent = lax.dynamic_index_in_dim(pair, 1 - side, 1, keepdims=False)
        parts = kept + lax.ppermute(sent, axis, [(s, s ^ bit) for s in range(count)])
        bit *= 2
    return parts[0]


def local(amp_traces, patch_owner, patch_fault, patch_trace, patch_offset):
    bricks, slabs = lax.axis_size("brick"), lax.axis_size("bulk")
    nx, strip, nt = amp_traces.shape
    cx, cy = nx // bricks, strip * bricks
    patches = patch_fault.shape[0]
    faults = slabs * F_DEV

    places = jnp.broadcast_to((patch_trace * nt + patch_offset)[:, None], (patches, LANES))
    pieces, layout, places = exchange_bricks(amp_traces, cx, places)
    low, high, _ = halo_columns(pieces, layout, cx, ())

    fault = patch_owner[:, 0] * F_DEV + patch_fault
    members = fault[None, :] == jnp.arange(faults, dtype=jnp.int32)[:, None]
    counts = jnp.sum(members.astype(jnp.float32), axis=1)
    members = members.astype(jnp.bfloat16)
    where = jnp.stack([
        lax.axis_index("brick"), lax.axis_index("bulk"), jnp.int32(bricks), jnp.int32(slabs)])

    halves = nt // LANES
    wide = cy + 8
    vmem = pl.BlockSpec(memory_space=pltpu.VMEM)
    anywhere = pl.BlockSpec(memory_space=pl.ANY)

    def kernel(*refs):
        brick_kernel(layout, strip, cx, cy, nt, patches, *refs)

    attribute, partial = pl.pallas_call(
        kernel,
        out_shape=(
            jax.ShapeDtypeStruct((cx * cy, nt), jnp.float32),
            jax.ShapeDtypeStruct((faults, PATCH), jnp.float32),
        ),
        in_specs=[pl.BlockSpec(memory_space=pltpu.SMEM)] + [vmem] * 5 + [anywhere] * (len(layout) + 1),
        out_specs=(anywhere, vmem),
        scratch_shapes=[
            pltpu.VMEM((halves, cx + 4 * RIM, cy + 2 * LEAD, LANES), jnp.float32),
            pltpu.VMEM((cx + 4, halves, wide, LANES), jnp.float32),
            pltpu.VMEM((cx + 4, halves, wide, LANES), jnp.float32),
            pltpu.VMEM((16, halves, wide, LANES), jnp.float32),
            pltpu.VMEM((4, 2, cx * cy, nt), jnp.bfloat16),
            pltpu.VMEM((cx * cy, 2 * nt), jnp.bfloat16),
            pltpu.VMEM((cx * cy, nt), jnp.float32),
            pltpu.VMEM((patches, LANES), jnp.int32),
            pltpu.VMEM((patches, 2 * PATCH), jnp.bfloat16),
            pltpu.SemaphoreType.DMA((len(layout) * halves + 2,)),
        ],
        compiler_params=pltpu.CompilerParams(vmem_limit_bytes=48 * 1024 * 1024),
        cost_estimate=pl.CostEstimate(flops=2_500_000_000, bytes_accessed=10_000_000, transcendentals=0),
        name="brick_attribute",
    )(where, low, high, band(nt, 2), band(nt, 4), members, *pieces, places)

    tally = jnp.pad(counts.reshape(slabs, 1, F_DEV), ((0, 0), (0, 0), (0, PATCH - F_DEV)))
    parts = jnp.concatenate([partial.reshape(slabs, F_DEV, PATCH), tally], axis=1)
    total = reduce_scatter(parts, "bulk")
    profile = total[:F_DEV] / jnp.maximum(total[F_DEV, :F_DEV], 1.0)[:, None]
    return attribute.reshape(cx, cy, nt), profile


def solution(mesh):
    in_specs = (
        P(None, ("bulk", "brick"), None),
        P(("brick", "bulk"), None),
        P(("brick", "bulk")),
        P(("brick", "bulk")),
        P(("brick", "bulk")),
    )
    out_specs = (P("brick", "bulk", None), P(("brick", "bulk"), None))
    return jax.shard_map(local, mesh=mesh, in_specs=in_specs, out_specs=out_specs, check_vma=False)
```

```python
import jax
import jax.numpy as jnp
from jax import lax
from jax.experimental import pallas as pl
from jax.experimental.pallas import tpu as pltpu
from jax.sharding import PartitionSpec as P

PATCH = 128
F_DEV = 16
RIM = 3
LEAD = 8
LANES = 128
TIES = (0, 0, 2)
WHICH = 2
BLOCK = 256


def split_bf16(values):
    high = values.astype(jnp.bfloat16)
    low = (values - high.astype(jnp.float32)).astype(jnp.bfloat16)
    return high, low


def dot(left, right):
    return jnp.dot(left, right, preferred_element_type=jnp.float32)


def brick_kernel(
    layout, strip, cx, cy, nt, patches,
    where_ref, low_ref, high_ref, band5_ref, band9_ref, faults_ref, *refs,
):
    pieces = refs[:len(layout)]
    places_hbm, attr_hbm, partial_ref = refs[len(layout):len(layout) + 3]
    amp, exy, ett, box, fields, rows_bf, attr, places, windows, early, sems = refs[len(layout) + 3:]
    halves = nt // LANES
    brick, slab, bricks, slabs = where_ref[0], where_ref[1], where_ref[2], where_ref[3]
    wide = cy + 8

    rows = cx + 2 * RIM
    top = jnp.where(brick == 0, 2 * RIM, jnp.where(brick == bricks - 1, 0, RIM))
    fetches = []
    for n, (d, part, width) in enumerate(layout):
        source = brick ^ d
        column = LEAD + strip * source + width * part_of(source, bricks, part)
        piece = pieces[n] if d else pieces[n].at[pl.ds(brick * cx + top - 2 * RIM, rows)]
        for h in range(halves):
            fetches.append(pltpu.make_async_copy(
                piece.at[:, :, pl.ds(h * LANES, LANES)],
                amp.at[h, pl.ds(top, rows), pl.ds(pl.multiple_of(column, 8), width), :],
                sems.at[n * halves + h],
            ))
    base = len(layout) * halves
    fetch_places = pltpu.make_async_copy(places_hbm, places, sems.at[base])
    for copy in fetches:
        copy.start()
    fetch_places.start()
    even = lax.rem(slab, 2) == 0
    for h in range(halves):
        lanes = pl.ds(h * LANES, LANES)
        near, far = low_ref[:, :, lanes], high_ref[:, :, lanes]
        amp[h, pl.ds(top, rows), LEAD - RIM:LEAD, :] = jnp.where(even, far, near)
        amp[h, pl.ds(top, rows), LEAD + cy:LEAD + cy + RIM, :] = jnp.where(even, near, far)
    for copy in fetches:
        copy.wait()

    @pl.when(brick == 0)
    def _():
        amp[:, RIM:2 * RIM] = jnp.zeros((halves, RIM) + amp.shape[2:], jnp.float32)

    @pl.when(brick == bricks - 1)
    def _():
        amp[:, cx + 2 * RIM:cx + 3 * RIM] = jnp.zeros((halves, RIM) + amp.shape[2:], jnp.float32)

    lane = lax.broadcasted_iota(jnp.int32, (wide, LANES), 1)
    first, last = lane == 0, lane == LANES - 1
    column = lax.broadcasted_iota(jnp.int32, (wide, LANES), 0)
    inside = jnp.logical_and(
        jnp.logical_or(slab > 0, column >= 2),
        jnp.logical_or(slab < slabs - 1, column < cy + 2),
    ).astype(jnp.float32)
    origin = LEAD - RIM

    def energy_row(e, carry):
        position = brick * cx + e - 2
        valid = jnp.logical_and(position >= 0, position < bricks * cx).astype(jnp.float32)
        mask = inside * valid
        centre = [amp[h, e + 1 + RIM, origin + 1:origin + 1 + wide, :] for h in range(halves)]
        back = [pltpu.roll(c, 1, 1) for c in centre]
        ahead = [pltpu.roll(c, LANES - 1, 1) for c in centre]
        for h in range(halves):
            slope_x = (amp[h, e + 2 + RIM, origin + 1:origin + 1 + wide, :]
                       - amp[h, e + RIM, origin + 1:origin + 1 + wide, :])
            slope_y = (amp[h, e + 1 + RIM, origin + 2:origin + 2 + wide, :]
                       - amp[h, e + 1 + RIM, origin:origin + wide, :])
            before = jnp.where(first, back[h - 1] if h > 0 else 0.0, back[h])
            after = jnp.where(last, ahead[h + 1] if h < halves - 1 else 0.0, ahead[h])
            slope_t = after - before
            exy[e, h] = (slope_x * slope_x + slope_y * slope_y) * mask
            ett[e, h] = slope_t * slope_t * mask
        return carry

    for e in range(cx // 2 + 4):
        energy_row(e, 0)

    def across(slot, h, radius, row):
        box[slot, h] = row
        total = box[slot, h, 0:cy, :]
        for j in range(1, 2 * radius + 1):
            total = total + box[slot, h, j:j + cy, :]
        return total

    def inline5(field, r, h):
        e = [field[r + j, h] for j in range(8)]
        low, middle, high = e[1] + e[2], e[3] + e[4], e[5] + e[6]
        left, right = low + middle, middle + high
        return left + e[0], left + e[5], right + e[2], right + e[7]

    def inline3(e):
        low, high = e[1] + e[2], e[3] + e[4]
        return low + e[0], low + e[3], high + e[2], high + e[5]

    def keep(index, at, h, values):
        high, low = split_bf16(values)
        fields[index, 0, at, h * LANES:(h + 1) * LANES] = high
        fields[index, 1, at, h * LANES:(h + 1) * LANES] = low

    def sum_rows(q, carry):
        r = 4 * q
        near = slice(LEAD - 1, LEAD - 1 + wide)
        for h in range(halves):
            rows = [amp[h, r + 2 * RIM - 1 + j, near, :] for j in range(6)]
            stacks = inline3(rows)
            powers = inline3([row * row for row in rows])
            xys, ts = inline5(exy, r, h), inline5(ett, r, h)
            for j in range(4):
                at = pl.ds((r + j) * cy, cy)
                keep(0, at, h, across(4 * j + 0, h, 2, xys[j]))
                keep(1, at, h, across(4 * j + 1, h, 2, ts[j]))
                stack = across(4 * j + 2, h, 1, stacks[j])
                power = 9.0 * across(4 * j + 3, h, 1, powers[j])
                keep(2, at, h, power - stack * stack)
                keep(3, at, h, power)
        return carry

    band5, band9 = band5_ref[...], band9_ref[...]
    half = cx * cy // 2
    lane_block = lax.broadcasted_iota(jnp.int32, (BLOCK, LANES), 1)

    def finish_half(j):
        at = pl.ds(j * half, half)
        sums = [dot(fields[f, 0, at, :], b) + dot(fields[f, 1, at, :], b)
                for f, b in enumerate((band5, band5, band9, band9))]
        both = (sums[3] + 1e-5) * (sums[0] + sums[1] + 4e-5)
        inverse = pl.reciprocal(both, approx=True)
        inverse = inverse * (2.0 - both * inverse)
        values = (sums[2] + 1e-5) * sums[0] * inverse
        attr[at, :] = values
        high, low = split_bf16(values)
        rows_bf[at, 0:nt] = high
        rows_bf[at, nt:2 * nt] = low

    def picked(n, j):
        at = pl.ds(n * BLOCK, BLOCK)
        place = places[at, :]
        trace = lax.shift_right_logical(place, nt.bit_length() - 1)
        chosen = dot(jnp.concatenate([
            (lane_block + k == trace).astype(jnp.float32).astype(jnp.bfloat16)
            for k in range(j * half, (j + 1) * half, LANES)], axis=1), rows_bf[pl.ds(j * half, half), :])
        return at, place - trace * nt, chosen[:, 0:nt] + chosen[:, nt:2 * nt]

    blocks, quads = patches // BLOCK, cx // 4
    for q in range(quads // 2):
        sum_rows(q, 0)
    finish_half(0)
    for e in range(cx // 2 + 4, cx + 4):
        energy_row(e, 0)
    fetch_places.wait()
    for q in range(quads // 2, quads):
        sum_rows(q, 0)
        for n in range(blocks * (q - quads // 2) * 2 // quads, blocks * (q - quads // 2 + 1) * 2 // quads):
            at, _, rows = picked(n, 0)
            early[at, :] = rows
    finish_half(1)
    store = pltpu.make_async_copy(attr, attr_hbm, sems.at[base + 1])
    store.start()
    for n in range(blocks):
        at, shift, rows = picked(n, 1)
        rows = rows + early[at, :]
        mixed = jnp.where(lane_block < shift, rows[:, LANES:nt], rows[:, 0:LANES])
        window = jnp.take_along_axis(mixed, (lane_block + shift) & (LANES - 1), axis=1)
        high, low = split_bf16(window)
        windows[at, 0:PATCH] = high
        windows[at, PATCH:2 * PATCH] = low
    sums = dot(faults_ref[...], windows[...])
    partial_ref[...] = sums[:, 0:PATCH] + sums[:, PATCH:2 * PATCH]
    store.wait()


def band(nt, radius):
    at = jnp.arange(nt, dtype=jnp.int32)
    return (jnp.abs(at[:, None] - at[None, :]) <= radius).astype(jnp.bfloat16)


def part_of(strip_index, bricks, part):
    if part is None:
        return 0
    upper = (strip_index >= bricks // 2).astype(jnp.int32) if hasattr(strip_index, "astype") else int(
        strip_index >= bricks // 2)
    return upper if part == 0 else 1 - upper


def exchange_bricks(amp, cx, prepared):
    bricks = lax.axis_size("brick")
    mine = lax.axis_index("brick")
    nx, strip, nt = amp.shape
    rows = cx + 2 * RIM
    parts, width = ((0, 1), strip // 2) if strip % 16 == 0 else ((None,), strip)
    order = (bricks - 1, *range(1, bricks - 1))
    pieces, layout = [], []

    def cut(source, d, begin, columns):
        first = jnp.clip((mine ^ d) * cx - RIM, 0, nx - rows)
        return lax.dynamic_slice(source, (first, begin, 0), (rows, columns, nt))

    def send(piece, d):
        return lax.ppermute(piece, "brick", [(s, s ^ d) for s in range(bricks)])

    source = amp
    for part in parts:
        begin = width * part_of(mine, bricks, part)
        for n, d in enumerate(order):
            piece = cut(source, d, begin, width)
            if part == 1:
                if n == WHICH:
                    piece, _, prepared = lax.optimization_barrier((piece, pieces[TIES[n]], prepared))
                else:
                    piece, _ = lax.optimization_barrier((piece, pieces[TIES[n]]))
            elif n == 0:
                source, piece = lax.optimization_barrier((amp, piece))
            pieces.append(send(piece, d))
            layout.append((d, part, width))
    pieces.append(amp)
    layout.append((0, None, strip))
    return pieces, layout, prepared


def halo_columns(pieces, layout, cx, prepared):
    bricks = lax.axis_size("brick")
    slabs = lax.axis_size("bulk")
    mine = lax.axis_index("brick")
    rows = cx + 2 * RIM
    left, right = 0.0, 0.0
    for piece, (d, part, width) in zip(pieces, layout):
        if d == 0:
            first = jnp.clip(mine * cx - RIM, 0, piece.shape[0] - rows)
            piece = lax.dynamic_slice_in_dim(piece, first, rows, axis=0)
        if part != 1:
            left = jnp.where((mine ^ d) == 0, piece[:, :RIM], left)
            right = jnp.where((mine ^ d) == bricks - 1, piece[:, width - RIM:], right)
    left, right, *prepared = lax.optimization_barrier((left, right, *prepared))
    even = lax.axis_index("bulk") % 2 == 0
    inner = [p for s in range(0, slabs - 1, 2) for p in ((s, s + 1), (s + 1, s))]
    outer = [p for s in range(1, slabs - 1, 2) for p in ((s, s + 1), (s + 1, s))]
    near, far = jnp.where(even, right, left), jnp.where(even, left, right)
    far = lax.ppermute(far, "bulk", outer)
    near = lax.ppermute(near, "bulk", inner)
    low, high = near, far
    return low, high, prepared


def reduce_scatter(parts, axis):
    count = lax.axis_size(axis)
    mine = lax.axis_index(axis)
    bit = 1
    while bit < count:
        pair = parts.reshape(parts.shape[0] // 2, 2, *parts.shape[1:])
        side = mine // bit % 2
        kept = lax.dynamic_index_in_dim(pair, side, 1, keepdims=False)
        sent = lax.dynamic_index_in_dim(pair, 1 - side, 1, keepdims=False)
        parts = kept + lax.ppermute(sent, axis, [(s, s ^ bit) for s in range(count)])
        bit *= 2
    return parts[0]


def local(amp_traces, patch_owner, patch_fault, patch_trace, patch_offset):
    bricks, slabs = lax.axis_size("brick"), lax.axis_size("bulk")
    nx, strip, nt = amp_traces.shape
    cx, cy = nx // bricks, strip * bricks
    patches = patch_fault.shape[0]
    faults = slabs * F_DEV

    places = jnp.broadcast_to((patch_trace * nt + patch_offset)[:, None], (patches, LANES))
    pieces, layout, places = exchange_bricks(amp_traces, cx, places)
    low, high, _ = halo_columns(pieces, layout, cx, ())

    fault = patch_owner[:, 0] * F_DEV + patch_fault
    members = fault[None, :] == jnp.arange(faults, dtype=jnp.int32)[:, None]
    counts = jnp.sum(members.astype(jnp.float32), axis=1)
    members = members.astype(jnp.bfloat16)
    where = jnp.stack([
        lax.axis_index("brick"), lax.axis_index("bulk"), jnp.int32(bricks), jnp.int32(slabs)])

    halves = nt // LANES
    wide = cy + 8
    vmem = pl.BlockSpec(memory_space=pltpu.VMEM)
    anywhere = pl.BlockSpec(memory_space=pl.ANY)

    def kernel(*refs):
        brick_kernel(layout, strip, cx, cy, nt, patches, *refs)

    attribute, partial = pl.pallas_call(
        kernel,
        out_shape=(
            jax.ShapeDtypeStruct((cx * cy, nt), jnp.float32),
            jax.ShapeDtypeStruct((faults, PATCH), jnp.float32),
        ),
        in_specs=[pl.BlockSpec(memory_space=pltpu.SMEM)] + [vmem] * 5 + [anywhere] * (len(layout) + 1),
        out_specs=(anywhere, vmem),
        scratch_shapes=[
            pltpu.VMEM((halves, cx + 4 * RIM, cy + 2 * LEAD, LANES), jnp.float32),
            pltpu.VMEM((cx + 4, halves, wide, LANES), jnp.float32),
            pltpu.VMEM((cx + 4, halves, wide, LANES), jnp.float32),
            pltpu.VMEM((16, halves, wide, LANES), jnp.float32),
            pltpu.VMEM((4, 2, cx * cy, nt), jnp.bfloat16),
            pltpu.VMEM((cx * cy, 2 * nt), jnp.bfloat16),
            pltpu.VMEM((cx * cy, nt), jnp.float32),
            pltpu.VMEM((patches, LANES), jnp.int32),
            pltpu.VMEM((patches, 2 * PATCH), jnp.bfloat16),
            pltpu.VMEM((patches, nt), jnp.float32),
            pltpu.SemaphoreType.DMA((len(layout) * halves + 2,)),
        ],
        compiler_params=pltpu.CompilerParams(vmem_limit_bytes=48 * 1024 * 1024),
        cost_estimate=pl.CostEstimate(flops=2_500_000_000, bytes_accessed=10_000_000, transcendentals=0),
        name="brick_attribute",
    )(where, low, high, band(nt, 2), band(nt, 4), members, *pieces, places)

    tally = jnp.pad(counts.reshape(slabs, 1, F_DEV), ((0, 0), (0, 0), (0, PATCH - F_DEV)))
    parts = jnp.concatenate([partial.reshape(slabs, F_DEV, PATCH), tally], axis=1)
    total = reduce_scatter(parts, "bulk")
    profile = total[:F_DEV] / jnp.maximum(total[F_DEV, :F_DEV], 1.0)[:, None]
    return attribute.reshape(cx, cy, nt), profile


def solution(mesh):
    in_specs = (
        P(None, ("bulk", "brick"), None),
        P(("brick", "bulk"), None),
        P(("brick", "bulk")),
        P(("brick", "bulk")),
        P(("brick", "bulk")),
    )
    out_specs = (P("brick", "bulk", None), P(("brick", "bulk"), None))
    return jax.shard_map(local, mesh=mesh, in_specs=in_specs, out_specs=out_specs, check_vma=False)
```

```python
import jax
import jax.numpy as jnp
from jax import lax
from jax.experimental import pallas as pl
from jax.experimental.pallas import tpu as pltpu
from jax.sharding import PartitionSpec as P

PATCH = 128
F_DEV = 16
RIM = 3
LEAD = 8
LANES = 128
TIES = (0, 0, 2)
WHICH = 2
BLOCK = 256


def split_bf16(values):
    high = values.astype(jnp.bfloat16)
    low = (values - high.astype(jnp.float32)).astype(jnp.bfloat16)
    return high, low


def dot(left, right):
    return jnp.dot(left, right, preferred_element_type=jnp.float32)


def brick_kernel(
    layout, strip, cx, cy, nt, patches,
    where_ref, low_ref, high_ref, band5_ref, band9_ref, faults_ref, *refs,
):
    pieces = refs[:len(layout)]
    places_hbm, attr_hbm, partial_ref = refs[len(layout):len(layout) + 3]
    amp, exy, ett, box, fields, rows_bf, attr, places, windows, early, sems = refs[len(layout) + 3:]
    halves = nt // LANES
    brick, slab, bricks, slabs = where_ref[0], where_ref[1], where_ref[2], where_ref[3]
    wide = cy + 8

    rows = cx + 2 * RIM
    top = jnp.where(brick == 0, 2 * RIM, jnp.where(brick == bricks - 1, 0, RIM))
    fetches = []
    for n, (d, part, width) in enumerate(layout):
        source = brick ^ d
        column = LEAD + strip * source + width * part_of(source, bricks, part)
        piece = pieces[n] if d else pieces[n].at[pl.ds(brick * cx + top - 2 * RIM, rows)]
        for h in range(halves):
            fetches.append(pltpu.make_async_copy(
                piece.at[:, :, pl.ds(h * LANES, LANES)],
                amp.at[h, pl.ds(top, rows), pl.ds(pl.multiple_of(column, 8), width), :],
                sems.at[n * halves + h],
            ))
    base = len(layout) * halves
    fetch_places = pltpu.make_async_copy(places_hbm, places, sems.at[base])
    for copy in fetches:
        copy.start()
    fetch_places.start()
    even = lax.rem(slab, 2) == 0
    for h in range(halves):
        lanes = pl.ds(h * LANES, LANES)
        near, far = low_ref[:, :, lanes], high_ref[:, :, lanes]
        amp[h, pl.ds(top, rows), LEAD - RIM:LEAD, :] = jnp.where(even, far, near)
        amp[h, pl.ds(top, rows), LEAD + cy:LEAD + cy + RIM, :] = jnp.where(even, near, far)
    for copy in fetches:
        copy.wait()

    @pl.when(brick == 0)
    def _():
        amp[:, RIM:2 * RIM] = jnp.zeros((halves, RIM) + amp.shape[2:], jnp.float32)

    @pl.when(brick == bricks - 1)
    def _():
        amp[:, cx + 2 * RIM:cx + 3 * RIM] = jnp.zeros((halves, RIM) + amp.shape[2:], jnp.float32)

    lane = lax.broadcasted_iota(jnp.int32, (wide, LANES), 1)
    first, last = lane == 0, lane == LANES - 1
    column = lax.broadcasted_iota(jnp.int32, (wide, LANES), 0)
    inside = jnp.logical_and(
        jnp.logical_or(slab > 0, column >= 2),
        jnp.logical_or(slab < slabs - 1, column < cy + 2),
    ).astype(jnp.float32)
    origin = LEAD - RIM

    def energy_row(e, carry):
        position = brick * cx + e - 2
        valid = jnp.logical_and(position >= 0, position < bricks * cx).astype(jnp.float32)
        mask = inside * valid
        centre = [amp[h, e + 1 + RIM, origin + 1:origin + 1 + wide, :] for h in range(halves)]
        back = [pltpu.roll(c, 1, 1) for c in centre]
        ahead = [pltpu.roll(c, LANES - 1, 1) for c in centre]
        for h in range(halves):
            slope_x = (amp[h, e + 2 + RIM, origin + 1:origin + 1 + wide, :]
                       - amp[h, e + RIM, origin + 1:origin + 1 + wide, :])
            slope_y = (amp[h, e + 1 + RIM, origin + 2:origin + 2 + wide, :]
                       - amp[h, e + 1 + RIM, origin:origin + wide, :])
            before = jnp.where(first, back[h - 1] if h > 0 else 0.0, back[h])
            after = jnp.where(last, ahead[h + 1] if h < halves - 1 else 0.0, ahead[h])
            slope_t = after - before
            across_xy = slope_x * slope_x + slope_y * slope_y
            along_t = slope_t * slope_t
            for field, values in ((exy, across_xy), (ett, along_t)):
                inner = values[8:cy]
                field[e, h, 0:8, :] = values[0:8] * mask[0:8]
                field[e, h, 8:cy, :] = inner if 2 <= e < cx + 2 else inner * mask[8:cy]
                field[e, h, cy:wide, :] = values[cy:wide] * mask[cy:wide]
        return carry

    for e in range(cx // 2 + 4):
        energy_row(e, 0)

    def across(slot, h, radius, row):
        box[slot, h] = row
        total = box[slot, h, 0:cy, :]
        for j in range(1, 2 * radius + 1):
            total = total + box[slot, h, j:j + cy, :]
        return total

    def inline5(field, r, h):
        e = [field[r + j, h] for j in range(8)]
        low, middle, high = e[1] + e[2], e[3] + e[4], e[5] + e[6]
        left, right = low + middle, middle + high
        return left + e[0], left + e[5], right + e[2], right + e[7]

    def inline3(e):
        low, high = e[1] + e[2], e[3] + e[4]
        return low + e[0], low + e[3], high + e[2], high + e[5]

    def keep(index, at, h, values):
        high, low = split_bf16(values)
        fields[index, 0, at, h * LANES:(h + 1) * LANES] = high
        fields[index, 1, at, h * LANES:(h + 1) * LANES] = low

    def sum_rows(q, carry):
        r = 4 * q
        near = slice(LEAD - 1, LEAD - 1 + wide)
        for h in range(halves):
            rows = [amp[h, r + 2 * RIM - 1 + j, near, :] for j in range(6)]
            stacks = inline3(rows)
            powers = inline3([row * row for row in rows])
            xys, ts = inline5(exy, r, h), inline5(ett, r, h)
            for j in range(4):
                at = pl.ds((r + j) * cy, cy)
                keep(0, at, h, across(4 * j + 0, h, 2, xys[j]))
                keep(1, at, h, across(4 * j + 1, h, 2, ts[j]))
                stack = across(4 * j + 2, h, 1, stacks[j])
                power = 9.0 * across(4 * j + 3, h, 1, powers[j])
                keep(2, at, h, power - stack * stack)
                keep(3, at, h, power)
        return carry

    band5, band9 = band5_ref[...], band9_ref[...]
    half = cx * cy // 2
    lane_block = lax.broadcasted_iota(jnp.int32, (BLOCK, LANES), 1)

    def finish_half(j):
        at = pl.ds(j * half, half)
        sums = [dot(fields[f, 0, at, :], b) + dot(fields[f, 1, at, :], b)
                for f, b in enumerate((band5, band5, band9, band9))]
        both = (sums[3] + 1e-5) * (sums[0] + sums[1] + 4e-5)
        inverse = pl.reciprocal(both, approx=True)
        inverse = inverse * (2.0 - both * inverse)
        values = (sums[2] + 1e-5) * sums[0] * inverse
        attr[at, :] = values
        high, low = split_bf16(values)
        rows_bf[at, 0:nt] = high
        rows_bf[at, nt:2 * nt] = low

    def picked(n, j):
        at = pl.ds(n * BLOCK, BLOCK)
        place = places[at, :]
        trace = lax.shift_right_logical(place, nt.bit_length() - 1)
        chosen = dot(jnp.concatenate([
            (lane_block + k == trace).astype(jnp.float32).astype(jnp.bfloat16)
            for k in range(j * half, (j + 1) * half, LANES)], axis=1), rows_bf[pl.ds(j * half, half), :])
        return at, place - trace * nt, chosen[:, 0:nt] + chosen[:, nt:2 * nt]

    blocks, quads = patches // BLOCK, cx // 4
    for q in range(quads // 2):
        sum_rows(q, 0)
    finish_half(0)
    for e in range(cx // 2 + 4, cx + 4):
        energy_row(e, 0)
    fetch_places.wait()
    for q in range(quads // 2, quads):
        sum_rows(q, 0)
        for n in range(blocks * (q - quads // 2) * 2 // quads, blocks * (q - quads // 2 + 1) * 2 // quads):
            at, _, rows = picked(n, 0)
            early[at, :] = rows
    finish_half(1)
    store = pltpu.make_async_copy(attr, attr_hbm, sems.at[base + 1])
    store.start()
    for n in range(blocks):
        at, shift, rows = picked(n, 1)
        rows = rows + early[at, :]
        mixed = jnp.where(lane_block < shift, rows[:, LANES:nt], rows[:, 0:LANES])
        window = jnp.take_along_axis(mixed, (lane_block + shift) & (LANES - 1), axis=1)
        high, low = split_bf16(window)
        windows[at, 0:PATCH] = high
        windows[at, PATCH:2 * PATCH] = low
    sums = dot(faults_ref[...], windows[...])
    partial_ref[...] = sums[:, 0:PATCH] + sums[:, PATCH:2 * PATCH]
    store.wait()


def band(nt, radius):
    at = jnp.arange(nt, dtype=jnp.int32)
    return (jnp.abs(at[:, None] - at[None, :]) <= radius).astype(jnp.bfloat16)


def part_of(strip_index, bricks, part):
    if part is None:
        return 0
    upper = (strip_index >= bricks // 2).astype(jnp.int32) if hasattr(strip_index, "astype") else int(
        strip_index >= bricks // 2)
    return upper if part == 0 else 1 - upper


def exchange_bricks(amp, cx, prepared):
    bricks = lax.axis_size("brick")
    mine = lax.axis_index("brick")
    nx, strip, nt = amp.shape
    rows = cx + 2 * RIM
    parts, width = ((0, 1), strip // 2) if strip % 16 == 0 else ((None,), strip)
    order = (bricks - 1, *range(1, bricks - 1))
    pieces, layout = [], []

    def cut(source, d, begin, columns):
        first = jnp.clip((mine ^ d) * cx - RIM, 0, nx - rows)
        return lax.dynamic_slice(source, (first, begin, 0), (rows, columns, nt))

    def send(piece, d):
        return lax.ppermute(piece, "brick", [(s, s ^ d) for s in range(bricks)])

    source = amp
    for part in parts:
        begin = width * part_of(mine, bricks, part)
        for n, d in enumerate(order):
            piece = cut(source, d, begin, width)
            if part == 1:
                if n == WHICH:
                    piece, _, prepared = lax.optimization_barrier((piece, pieces[TIES[n]], prepared))
                else:
                    piece, _ = lax.optimization_barrier((piece, pieces[TIES[n]]))
            elif n == 0:
                source, piece = lax.optimization_barrier((amp, piece))
            pieces.append(send(piece, d))
            layout.append((d, part, width))
    pieces.append(amp)
    layout.append((0, None, strip))
    return pieces, layout, prepared


def halo_columns(pieces, layout, cx, prepared):
    bricks = lax.axis_size("brick")
    slabs = lax.axis_size("bulk")
    mine = lax.axis_index("brick")
    rows = cx + 2 * RIM
    left, right = 0.0, 0.0
    for piece, (d, part, width) in zip(pieces, layout):
        if d == 0:
            first = jnp.clip(mine * cx - RIM, 0, piece.shape[0] - rows)
            piece = lax.dynamic_slice_in_dim(piece, first, rows, axis=0)
        if part != 1:
            left = jnp.where((mine ^ d) == 0, piece[:, :RIM], left)
            right = jnp.where((mine ^ d) == bricks - 1, piece[:, width - RIM:], right)
    left, right, *prepared = lax.optimization_barrier((left, right, *prepared))
    even = lax.axis_index("bulk") % 2 == 0
    inner = [p for s in range(0, slabs - 1, 2) for p in ((s, s + 1), (s + 1, s))]
    outer = [p for s in range(1, slabs - 1, 2) for p in ((s, s + 1), (s + 1, s))]
    near, far = jnp.where(even, right, left), jnp.where(even, left, right)
    far = lax.ppermute(far, "bulk", outer)
    near = lax.ppermute(near, "bulk", inner)
    low, high = near, far
    return low, high, prepared


def reduce_scatter(parts, axis):
    count = lax.axis_size(axis)
    mine = lax.axis_index(axis)
    bit = 1
    while bit < count:
        pair = parts.reshape(parts.shape[0] // 2, 2, *parts.shape[1:])
        side = mine // bit % 2
        kept = lax.dynamic_index_in_dim(pair, side, 1, keepdims=False)
        sent = lax.dynamic_index_in_dim(pair, 1 - side, 1, keepdims=False)
        parts = kept + lax.ppermute(sent, axis, [(s, s ^ bit) for s in range(count)])
        bit *= 2
    return parts[0]


def local(amp_traces, patch_owner, patch_fault, patch_trace, patch_offset):
    bricks, slabs = lax.axis_size("brick"), lax.axis_size("bulk")
    nx, strip, nt = amp_traces.shape
    cx, cy = nx // bricks, strip * bricks
    patches = patch_fault.shape[0]
    faults = slabs * F_DEV

    places = jnp.broadcast_to((patch_trace * nt + patch_offset)[:, None], (patches, LANES))
    pieces, layout, places = exchange_bricks(amp_traces, cx, places)
    low, high, _ = halo_columns(pieces, layout, cx, ())

    fault = patch_owner[:, 0] * F_DEV + patch_fault
    members = fault[None, :] == jnp.arange(faults, dtype=jnp.int32)[:, None]
    counts = jnp.sum(members.astype(jnp.float32), axis=1)
    members = members.astype(jnp.bfloat16)
    where = jnp.stack([
        lax.axis_index("brick"), lax.axis_index("bulk"), jnp.int32(bricks), jnp.int32(slabs)])

    halves = nt // LANES
    wide = cy + 8
    vmem = pl.BlockSpec(memory_space=pltpu.VMEM)
    anywhere = pl.BlockSpec(memory_space=pl.ANY)

    def kernel(*refs):
        brick_kernel(layout, strip, cx, cy, nt, patches, *refs)

    attribute, partial = pl.pallas_call(
        kernel,
        out_shape=(
            jax.ShapeDtypeStruct((cx * cy, nt), jnp.float32),
            jax.ShapeDtypeStruct((faults, PATCH), jnp.float32),
        ),
        in_specs=[pl.BlockSpec(memory_space=pltpu.SMEM)] + [vmem] * 5 + [anywhere] * (len(layout) + 1),
        out_specs=(anywhere, vmem),
        scratch_shapes=[
            pltpu.VMEM((halves, cx + 4 * RIM, cy + 2 * LEAD, LANES), jnp.float32),
            pltpu.VMEM((cx + 4, halves, wide, LANES), jnp.float32),
            pltpu.VMEM((cx + 4, halves, wide, LANES), jnp.float32),
            pltpu.VMEM((16, halves, wide, LANES), jnp.float32),
            pltpu.VMEM((4, 2, cx * cy, nt), jnp.bfloat16),
            pltpu.VMEM((cx * cy, 2 * nt), jnp.bfloat16),
            pltpu.VMEM((cx * cy, nt), jnp.float32),
            pltpu.VMEM((patches, LANES), jnp.int32),
            pltpu.VMEM((patches, 2 * PATCH), jnp.bfloat16),
            pltpu.VMEM((patches, nt), jnp.float32),
            pltpu.SemaphoreType.DMA((len(layout) * halves + 2,)),
        ],
        compiler_params=pltpu.CompilerParams(vmem_limit_bytes=32 * 1024 * 1024),
        cost_estimate=pl.CostEstimate(flops=2_500_000_000, bytes_accessed=10_000_000, transcendentals=0),
        name="brick_attribute",
    )(where, low, high, band(nt, 2), band(nt, 4), members, *pieces, places)

    tally = jnp.pad(counts.reshape(slabs, 1, F_DEV), ((0, 0), (0, 0), (0, PATCH - F_DEV)))
    parts = jnp.concatenate([partial.reshape(slabs, F_DEV, PATCH), tally], axis=1)
    total = reduce_scatter(parts, "bulk")
    profile = total[:F_DEV] / jnp.maximum(total[F_DEV, :F_DEV], 1.0)[:, None]
    return attribute.reshape(cx, cy, nt), profile


def solution(mesh):
    in_specs = (
        P(None, ("bulk", "brick"), None),
        P(("brick", "bulk"), None),
        P(("brick", "bulk")),
        P(("brick", "bulk")),
        P(("brick", "bulk")),
    )
    out_specs = (P("brick", "bulk", None), P(("brick", "bulk"), None))
    return jax.shard_map(local, mesh=mesh, in_specs=in_specs, out_specs=out_specs, check_vma=False)
```
